32 devices in a mesh: grp: 4 (over z), dev: 8 (over y, x, core).
Axes of the slice: x: 2, y: 2, z: 4, core: 2. Of those that a mesh axis runs over, the one named last changes fastest.
Arguments:
- particles: bfloat16 [512, 2, 6144], P(('grp', 'dev')), may hold values from -24 to 24
- defocus_bin: int32 [512], P(('grp', 'dev')), may hold values from 0 to 15
- candidates: int32 [512, 8], P(('grp', 'dev')), may hold values from 0 to 15, as said below
- projections: bfloat16 [16, 2, 6144], P('dev'), may hold values from -1 to 1
- ctf_table: bfloat16 [16, 6144], replicated, may hold values from -1 to 1
- inv_noise: float32 [6144], replicated, may hold values from 0.25 to 4
- line_slab: int32 [16, 48], P('dev'), may hold values from 0 to 3, as said below
- slab_owner: int32 [4], replicated, may hold values from 0 to 3, each once
Outputs:
- slab_data: float32 [4, 16, 2, 24, 128], P('grp', 'dev')
- slab_weight: float32 [4, 16, 24, 128], P('grp', 'dev')
The draws below stay inside these ranges and needn't reach their ends.
Inputs may be any that keep to these rules, and one draw needn't show every extreme that they name: `candidates`: each particle lists 8 different projections. `line_slab`: no slab holds more than 24 lines of one projection, and for every projection one slab holds exactly 24 of them. `slab_owner`: each group owns exactly one slab.
All inputs are finite; a program needn't handle non-finite values.
Results may differ from the reference program's by a relative error of at most 0.02.
Values may be sent and summed in bfloat16 or wider, within the bound.
No kernel may reach another device: no remote copies, remote signals or barrier semaphores. Data moves between devices by JAX's collectives and lax.ppermute only.
A program may use at most 64 MiB of HBM per device.

```python
import math
import jax
import jax.numpy as jnp
from jax import lax

LINE_LEN = 128
NUM_LINES = 48
PIXELS = 6144
PART_DEV = 16
PARTICLES = 512
PROJECTIONS = 16
SHIFTS = 9
CANDIDATES = 8
DEFOCUS_BINS = 16
SLABS = 4
CAPACITY = 24
N_GRP = 4
N_DEV = 8


def projection_scales(key):
    spread = jax.random.uniform(jax.random.fold_in(key, 102), (PROJECTIONS,), jnp.float32, math.log(0.5), math.log(2.0))
    return jnp.exp(spread)


def projection_values(key):
    base = jax.random.fold_in(key, 101)
    shape = (PROJECTIONS, 2, PIXELS)
    values = jnp.clip(jax.random.normal(base, shape, jnp.float32), -5.0, 5.0)
    amplitude = projection_scales(key)
    return values * amplitude[:, None, None] * (1.0 / math.sqrt(PIXELS))


def ctf_values(key):
    values = jax.random.uniform(jax.random.fold_in(key, 202), (DEFOCUS_BINS, PIXELS), jnp.float32, -1.0, 1.0)
    return values


def bin_values(key):
    return jax.random.randint(jax.random.fold_in(key, 303), (PARTICLES,), 0, DEFOCUS_BINS, dtype=jnp.int32)


def candidate_values(key):
    raw_scores = jax.random.randint(jax.random.fold_in(key, 404), (PARTICLES, PROJECTIONS), 0, 1 << 20, dtype=jnp.int32)
    raw_scores = raw_scores * PROJECTIONS + jnp.arange(PROJECTIONS, dtype=jnp.int32)[None, :]
    picked = lax.top_k(raw_scores, CANDIDATES)[1]
    return picked.astype(jnp.int32)


def draw_projections(key, part):
    return projection_values(key).astype(jnp.bfloat16)


def draw_ctf_table(key, part):
    return ctf_values(key).astype(jnp.bfloat16)


def draw_defocus_bin(key, part):
    return bin_values(key)


def draw_candidates(key, part):
    return candidate_values(key)


def draw_particles(key, part):
    base = jax.random.fold_in(key, 505)
    shape = (PARTICLES, 2, PIXELS)
    noise = jax.random.normal(base, shape, jnp.float32)
    return jnp.clip(noise, -24.0, 24.0).astype(jnp.bfloat16)


def draw_line_slab(key, part):
    row_keys = jax.random.split(jax.random.fold_in(key, 606), PROJECTIONS)

    def one_row(row_key):
        pick_key, mix_key, order_key = jax.random.split(row_key, 3)
        hottest = jax.random.randint(pick_key, (), 0, SLABS, dtype=jnp.int32)
        label_pool = jnp.arange(SLABS * CAPACITY, dtype=jnp.int32) // CAPACITY
        others = jax.random.permutation(mix_key, label_pool[CAPACITY:])[:NUM_LINES - CAPACITY]
        labels = jnp.concatenate([jnp.zeros((CAPACITY,), jnp.int32), others])
        labels = (labels + hottest) % SLABS
        return jax.random.permutation(order_key, labels)
    return jax.vmap(one_row)(row_keys)


def setup_inputs(seed: int = 0) -> dict:
    arg_keys = jax.random.split(jax.random.key(seed), 9)
    return {
        "particles": draw_particles(jax.random.fold_in(arg_keys[8], 71), 0),
        "defocus_bin": draw_defocus_bin(jax.random.fold_in(arg_keys[8], 71), 0),
        "candidates": draw_candidates(jax.random.fold_in(arg_keys[8], 71), 0),
        "projections": draw_projections(jax.random.fold_in(arg_keys[8], 71), 0),
        "ctf_table": draw_ctf_table(jax.random.fold_in(arg_keys[8], 71), 0),
        "inv_noise": jnp.clip(jnp.exp(jax.random.uniform(arg_keys[5], (PIXELS,), jnp.float32, math.log(0.25), math.log(4.0))), 0.25, 4.0),
        "line_slab": draw_line_slab(jax.random.fold_in(arg_keys[8], 71), 0),
        "slab_owner": jax.random.permutation(arg_keys[7], SLABS).astype(jnp.int32),
    }


two_pi = 2.0 * math.pi
exact = lax.Precision.HIGHEST


def phase_tables():
    pixel_index = jnp.arange(PIXELS, dtype=jnp.int32)
    line_pos = (pixel_index // LINE_LEN).astype(jnp.float32)
    column = pixel_index % LINE_LEN
    frequency = jnp.where(column < LINE_LEN // 2, column, column - LINE_LEN).astype(jnp.float32)
    shift_index = jnp.arange(SHIFTS, dtype=jnp.int32)
    move_x = (shift_index // 3 - 1).astype(jnp.float32)
    move_y = (shift_index % 3 - 1).astype(jnp.float32)
    angles = (move_x[:, None] * line_pos[None, :] + move_y[:, None] * frequency[None, :]) * (two_pi / LINE_LEN)
    return jnp.cos(angles), jnp.sin(angles)


def slot_tables(line_slab, slab_owner):
    slab_ids = jnp.arange(SLABS, dtype=jnp.int32)
    slab_hit = line_slab[:, :, None] == slab_ids[None, None, :]
    owner_line = jnp.sum(jnp.where(slab_hit, slab_owner[None, None, :], 0), axis=2).astype(jnp.int32)
    line_ids = jnp.arange(NUM_LINES, dtype=jnp.int32)
    earlier = line_ids[None, :] < line_ids[:, None]
    same_owner = owner_line[:, :, None] == owner_line[:, None, :]
    line_rank = jnp.sum(jnp.logical_and(same_owner, earlier[None]), axis=2).astype(jnp.int32)
    return owner_line, line_rank


def reference(particles, defocus_bin, candidates, projections, ctf_table, inv_noise, line_slab, slab_owner):
    cosines, sine_table = phase_tables()
    table_values = ctf_table.astype(jnp.float32)
    ctf_square = table_values * table_values
    noisy_square = ctf_square * inv_noise[None, :]
    proj_values = projections.astype(jnp.float32)
    pix_power = proj_values[:, 0] * proj_values[:, 0] + proj_values[:, 1] * proj_values[:, 1]
    bin_power = jnp.dot(noisy_square, pix_power.T, precision=exact)
    real_shift = proj_values[None, :, 0] * cosines[:, None, :] - proj_values[None, :, 1] * sine_table[:, None, :]
    imag_shift = proj_values[None, :, 0] * sine_table[:, None, :] + proj_values[None, :, 1] * cosines[:, None, :]
    shifted = jnp.concatenate([real_shift, imag_shift], axis=2)
    shifted = lax.optimization_barrier(shifted.astype(jnp.bfloat16)).astype(jnp.float32)

    blocks = N_GRP * N_DEV
    device_blocks = particles.reshape(blocks, PART_DEV, 2, PIXELS)
    bin_blocks = defocus_bin.reshape(blocks, PART_DEV)
    cand_blocks = candidates.reshape(blocks, PART_DEV, CANDIDATES)
    proj_ids = jnp.arange(PROJECTIONS, dtype=jnp.int32)
    bin_ids = jnp.arange(DEFOCUS_BINS, dtype=jnp.int32)

    def one_device(carry, inputs):
        data_sum, bin_sum = carry
        block, block_bins, block_cands = inputs
        onehot = (block_bins[:, None] == bin_ids[None, :]).astype(jnp.float32)
        ctf_rows = jnp.dot(onehot, table_values, precision=exact)
        images = block.astype(jnp.float32)
        weighted = (inv_noise[None, :] * ctf_rows)[:, None, :] * images
        weighted = lax.optimization_barrier(weighted.astype(jnp.bfloat16)).astype(jnp.float32)
        weighted = weighted.reshape(PART_DEV, 2 * PIXELS)
        scored = jnp.einsum("ik,tjk->itj", weighted, shifted, precision=exact)
        quad_term = jnp.dot(onehot, bin_power, precision=exact)
        scores = scored - 0.5 * quad_term[:, None, :]
        listed = jnp.any(block_cands[:, :, None] == proj_ids[None, None, :], axis=1)
        masked = jnp.where(listed[:, None, :], scores, -jnp.inf)
        row_peak = jnp.max(masked, axis=(1, 2), keepdims=True)
        exp_terms = jnp.exp(masked - row_peak)
        posterior = exp_terms / jnp.sum(exp_terms, axis=(1, 2), keepdims=True)
        post_low = lax.optimization_barrier(posterior.astype(jnp.bfloat16)).astype(jnp.float32)
        ctf_image = ctf_rows[:, None, :] * images
        ctf_image = lax.optimization_barrier(ctf_image.astype(jnp.bfloat16)).astype(jnp.float32)
        ctf_image = ctf_image.reshape(PART_DEV, 2 * PIXELS)
        summed = jnp.einsum("itj,ik->tjk", post_low, ctf_image, precision=exact)
        real_sum = summed[:, :, :PIXELS]
        imag_sum = summed[:, :, PIXELS:]
        data_real = jnp.sum(real_sum * cosines[:, None, :] + imag_sum * sine_table[:, None, :], axis=0)
        data_imag = jnp.sum(imag_sum * cosines[:, None, :] - real_sum * sine_table[:, None, :], axis=0)
        device_slice = jnp.stack([data_real, data_imag], axis=1)
        device_slice = lax.optimization_barrier(device_slice.astype(jnp.bfloat16)).astype(jnp.float32)
        proj_share = jnp.sum(posterior, axis=1)
        bin_share = jnp.dot(proj_share.T, onehot, precision=exact)
        return (data_sum + device_slice, bin_sum + bin_share), None

    start_data = jnp.zeros((PROJECTIONS, 2, PIXELS), jnp.float32)
    start_bins = jnp.zeros((PROJECTIONS, DEFOCUS_BINS), jnp.float32)
    (slice_data, bin_total), _ = lax.scan(one_device, (start_data, start_bins), (device_blocks, bin_blocks, cand_blocks))
    slice_weight = jnp.dot(bin_total, ctf_square, precision=exact) * (PROJECTIONS / PARTICLES)

    data_lines = slice_data.reshape(PROJECTIONS, 2, NUM_LINES, LINE_LEN)
    weight_lines = slice_weight.reshape(PROJECTIONS, NUM_LINES, LINE_LEN)
    owner_line, line_rank = slot_tables(line_slab, slab_owner)
    group_ids = jnp.arange(SLABS, dtype=jnp.int32)
    slot_ids = jnp.arange(CAPACITY, dtype=jnp.int32)
    selector = jnp.logical_and(owner_line[None, :, None, :] == group_ids[:, None, None, None], line_rank[None, :, None, :] == slot_ids[None, None, :, None]).astype(jnp.float32)
    slab_data = jnp.einsum("ojcl,jxlp->ojxcp", selector, data_lines, precision=exact)
    slab_weight = jnp.einsum("ojcl,jlp->ojcp", selector, weight_lines, precision=exact)
    return slab_data, slab_weight
```

```python
import functools
import math

import jax
import jax.numpy as jnp
import numpy as np
from jax import lax
from jax.experimental import pallas as pl
from jax.experimental.pallas import tpu as pltpu
from jax.sharding import PartitionSpec as P

LINE_LEN = 128
VMEM_BYTES = 40 * 1024 * 1024
f32 = jnp.float32
bf16 = jnp.bfloat16
exact = lax.Precision.HIGHEST
last_last = (((1,), (1,)), ((), ()))
first_first = (((0,), (0,)), ((), ()))


def trig_rows(pixels):
    k = np.arange(pixels)
    line = k // LINE_LEN
    column = k % LINE_LEN
    freq = np.where(column < LINE_LEN // 2, column, column - LINE_LEN)
    step = 2.0 * math.pi / LINE_LEN
    rows = np.zeros((8, pixels), np.float32)
    rows[0] = np.cos(line * step)
    rows[1] = np.sin(line * step)
    rows[2] = np.cos(freq * step)
    rows[3] = np.sin(freq * step)
    return rows


def call(kernel, out_shape, flops=0, moved=0, **kw):
    return pl.pallas_call(
        kernel,
        out_shape=out_shape,
        compiler_params=pltpu.CompilerParams(vmem_limit_bytes=VMEM_BYTES),
        cost_estimate=pl.CostEstimate(flops=flops, bytes_accessed=moved, transcendentals=0),
        **kw,
    )


def split(x):
    hi = x.astype(bf16)
    return hi, (x - hi.astype(f32)).astype(bf16)


def prep_kernel(part_ref, ints_ref, table_ref, trig_ref, y_ref):
    n = ints_ref.shape[0]
    bins = table_ref.shape[0]
    pixels = part_ref.shape[1]
    hit = ints_ref[:, 0:1] == lax.broadcasted_iota(jnp.int32, (n, bins), 1)
    onehot = hit.astype(f32).astype(bf16)
    width = 1024
    for c in range(pixels // width):
        cols = slice(c * width, (c + 1) * width)
        ctf = jnp.dot(onehot, table_ref[:, cols], preferred_element_type=f32)
        for part in range(2):
            x = part_ref[part * n : (part + 1) * n, cols].astype(f32) * ctf
            base = part * n
            y_ref[base : base + n, cols] = x.astype(bf16)
            y_ref[2 * n + base : 3 * n + base, cols] = (x * trig_ref[0:1, cols]).astype(bf16)
            y_ref[4 * n + base : 5 * n + base, cols] = (x * trig_ref[1:2, cols]).astype(bf16)


def score_kernel(chunks, rows, *refs):
    p_refs = refs[:chunks]
    (y0_ref, y1_ref, i0_ref, i1_ref, table_ref, noise_ref, trig_ref, pid_ref) = refs[
        chunks : chunks + 8
    ]
    m0_ref, m1_ref, s_ref, stat_ref = refs[chunks + 8 : chunks + 12]
    r_ref, q_ref = refs[chunks + 12 :]
    n = i0_ref.shape[0]
    bins = table_ref.shape[0]
    pixels = table_ref.shape[1]
    wide = 4 * chunks
    width = 1024
    if rows > 5 * wide:
        r_ref[5 * wide :, :] = jnp.zeros((rows - 5 * wide, pixels), bf16)
    for c in range(pixels // width):
        cols = slice(c * width, (c + 1) * width)
        x = jnp.concatenate([p[:, cols].astype(f32) for p in p_refs], axis=0)
        one = x * noise_ref[:, cols]
        r_ref[0:wide, cols] = one.astype(bf16)
        r_ref[wide : 2 * wide, cols] = (one * trig_ref[2:3, cols]).astype(bf16)
        r_ref[2 * wide : 3 * wide, cols] = (one * trig_ref[3:4, cols]).astype(bf16)
        high, low = split(one * x)
        r_ref[3 * wide : 4 * wide, cols] = high
        r_ref[4 * wide : 5 * wide, cols] = low
        t = table_ref[:, cols].astype(f32)
        high, low = split(t * t)
        q_ref[0:bins, cols] = high
        q_ref[bins : 2 * bins, cols] = low
    g0 = lax.dot_general(y0_ref[...], r_ref[...], last_last, preferred_element_type=f32)
    g1 = lax.dot_general(y1_ref[...], r_ref[...], last_last, preferred_element_type=f32)
    gq = lax.dot_general(q_ref[...], r_ref[...], last_last, preferred_element_type=f32)

    def left(v, k):
        return pltpu.roll(v, rows - k, 1)

    def right(v, k):
        return pltpu.roll(v, k, 1)

    lane = lax.broadcasted_iota(jnp.int32, (1, rows), 1)
    is_real = (lane % 4) < 2
    block0 = jnp.logical_and(is_real, lane < wide)
    block1 = jnp.logical_and(is_real, jnp.logical_and(lane >= wide, lane < 2 * wide))
    power = gq[:bins] + gq[bins:]
    power = power + left(power, wide)
    power = power + left(power, 2)
    power = jnp.where(block0, left(power, 3 * wide), jnp.where(block1, left(power, 2 * wide), 0.0))

    def take(part, a):
        base = (2 * a + part) * n
        return jnp.concatenate([g0[base : base + n], g1[base : base + n]], axis=0)

    even, odd = [], []
    for a in range(3):
        real, imag = take(0, a), take(1, a)
        even.append(real + left(imag, 2))
        odd.append(imag - left(real, 2))
    ints = jnp.concatenate([i0_ref[...], i1_ref[...]], axis=0)
    onehot = (ints[:, 0:1] == lax.broadcasted_iota(jnp.int32, (2 * n, bins), 1)).astype(f32)
    quad = 0.5 * jnp.dot(onehot, power, precision=exact, preferred_element_type=f32)
    pid = pid_ref[...]
    listed = ints[:, 1:2] == pid
    for c in range(2, 9):
        listed = jnp.logical_or(listed, ints[:, c : c + 1] == pid)
    valid1 = jnp.logical_and(listed, block1)
    valid01 = jnp.logical_and(listed, jnp.logical_or(block0, block1))

    base = [even[0] - quad, even[1] + odd[2] - quad, even[1] - odd[2] - quad]
    turn = [left(odd[0], wide), left(odd[1] - even[2], wide), left(odd[1] + even[2], wide)]
    plus = [b + jnp.where(block1, d, 0.0) for b, d in zip(base, turn)]
    minus = [b - d for b, d in zip(base, turn)]
    low = -3.0e38
    plus = [jnp.where(valid01, v, low) for v in plus]
    minus = [jnp.where(valid1, v, low) for v in minus]
    peak = plus[0]
    for v in plus[1:] + minus:
        peak = jnp.maximum(peak, v)
    peak = jnp.max(peak, axis=1, keepdims=True)
    plus = [jnp.where(valid01, jnp.exp(v - peak), 0.0) for v in plus]
    minus = [jnp.where(valid1, jnp.exp(v - peak), 0.0) for v in minus]
    both = [u + v for u, v in zip(plus, minus)]
    diff = [jnp.where(block1, u - v, 0.0) for u, v in zip(plus, minus)]
    total = both[0] + both[1] + both[2]
    mass = jnp.sum(total, axis=1, keepdims=True)
    lanes = lax.broadcasted_iota(jnp.int32, (2 * n, LINE_LEN), 1)
    stat_ref[...] = jnp.where(lanes == 0, peak, jnp.where(lanes == 1, mass, 0.0))
    s_ref[...] = jnp.where(block0, total + left(total, wide), 0.0)
    alpha = [both[0], both[1] + both[2], right(diff[2] - diff[1], wide)]
    beta = [right(diff[0], wide), right(diff[1] + diff[2], wide), both[1] - both[2]]
    for a in range(3):
        real = alpha[a] - right(beta[a], 2)
        imag = beta[a] + right(alpha[a], 2)
        for h, ref in enumerate((m0_ref, m1_ref)):
            ref[(2 * a) * n : (2 * a + 1) * n] = real[h * n : (h + 1) * n]
            ref[(2 * a + 1) * n : (2 * a + 2) * n] = imag[h * n : (h + 1) * n]


def slice_kernel(chunks, *refs):
    (y0_ref, y1_ref, m0_ref, m1_ref, s_ref, stat_ref, other_ref, i0_ref, i1_ref, trig_ref) = refs[:10]
    outs = refs[10:]
    n = i0_ref.shape[0]
    pixels = y0_ref.shape[1]
    wide = 4 * chunks
    other = jnp.concatenate([other_ref[n:], other_ref[:n]], axis=0)
    peak0, mass0 = stat_ref[:, 0:1], stat_ref[:, 1:2]
    peak1, mass1 = other[:, 0:1], other[:, 1:2]
    peak = jnp.maximum(peak0, peak1)
    grow = jnp.exp(peak0 - peak)
    scale = grow / (mass0 * grow + mass1 * jnp.exp(peak1 - peak))
    ints = jnp.concatenate([i0_ref[...], i1_ref[...]], axis=0)
    onehot = (ints[:, 0:1] == lax.broadcasted_iota(jnp.int32, (2 * n, LINE_LEN), 1)).astype(f32)
    share = lax.dot_general(
        s_ref[...] * scale, onehot, first_first, precision=exact, preferred_element_type=f32
    )[:wide].astype(bf16)
    mats = []
    for h, ref in enumerate((m0_ref, m1_ref)):
        part = scale[h * n : (h + 1) * n]
        m = ref[...] * jnp.concatenate([part] * 6, axis=0)
        mats.append(jnp.transpose(m)[: 3 * wide].astype(bf16))
    width = 1024
    for c in range(pixels // width):
        cols = slice(c * width, (c + 1) * width)
        x = jnp.dot(mats[0], y0_ref[:, cols], preferred_element_type=f32)
        x = x + jnp.dot(mats[1], y1_ref[:, cols], preferred_element_type=f32)
        x = (
            x[:wide]
            + x[wide : 2 * wide] * trig_ref[2:3, cols]
            + x[2 * wide :] * trig_ref[3:4, cols]
        )
        for s in range(chunks):
            outs[s][:, cols] = x[4 * s : 4 * s + 4].astype(bf16)
    for s in range(chunks):
        outs[s][:, pixels:] = share[4 * s : 4 * s + 4]


def pack_kernel(chunks, lines, cap, idx_ref, *refs):
    p_refs = refs[:chunks]
    keep_ref, send_ref = refs[chunks : chunks + 2]
    (scr_ref,) = refs[chunks + 2 :]
    half = keep_ref.shape[0] - 16
    scr_ref[...] = jnp.zeros(scr_ref.shape, f32)
    for l in range(lines + 1):
        cols = slice(l * LINE_LEN, (l + 1) * LINE_LEN)
        x = p_refs[0][:, cols].astype(f32)
        for p in p_refs[1:]:
            x = x + p[:, cols].astype(f32)
        if l < lines:
            for j in range(2):
                row = idx_ref[j, l]
                scr_ref[pl.ds(row, 1), :] = x[j : j + 1]
                scr_ref[pl.ds(row + cap, 1), :] = x[2 + j : 3 + j]
        else:
            tail = jnp.concatenate([x, jnp.zeros((12, LINE_LEN), f32)], axis=0)
    keep_ref[:half] = scr_ref[:half]
    keep_ref[half:] = tail
    send_ref[:half] = scr_ref[half:].astype(bf16)
    send_ref[half:] = tail.astype(bf16)


def table_kernel(lines, cap, idx_ref, table_ref, sel_ref):
    bins = table_ref.shape[0]
    sel_ref[...] = jnp.zeros(sel_ref.shape, f32)
    for l in range(lines):
        t = table_ref[:, l * LINE_LEN : (l + 1) * LINE_LEN].astype(f32)
        t = t * t
        for j in range(2):
            slot = idx_ref[j, l]

            @pl.when(slot < 4 * cap)
            def _():
                sel_ref[j, pl.ds(slot - 2 * cap * j, 1)] = t[None]


def final_kernel(cap, scale, acc_ref, recv_ref, bins_ref, sel_ref, data_ref, weight_ref):
    rows = 4 * cap
    x = acc_ref[...] + recv_ref[:rows].astype(f32)
    data_ref[...] = x.reshape(data_ref.shape)
    b = (bins_ref[...] + recv_ref[rows:].astype(f32)) * scale
    bt = jnp.transpose(b)[: sel_ref.shape[2]]
    for j in range(2):
        weight_ref[0, j] = jnp.sum(sel_ref[j] * bt[:, j : j + 1][None], axis=1)


def body(
    particles, defocus_bin, candidates, projections, ctf_table, inv_noise, line_slab, slab_owner
):
    n, _, pixels = particles.shape
    groups = lax.axis_size("grp")
    members = lax.axis_size("dev")
    chunks = members // 2
    lines = line_slab.shape[1]
    cap = 2 * lines // groups
    bins = ctf_table.shape[0]
    wide = 4 * chunks
    rows = -(-5 * wide // 128) * 128
    dev = lax.axis_index("dev")
    grp = lax.axis_index("grp")
    trig = jnp.asarray(trig_rows(pixels))
    noise = inv_noise[None, :]

    def swap(x, axis, size, mask):
        return lax.ppermute(x, axis, [(i, i ^ mask) for i in range(size)])

    own = jnp.transpose(projections, (1, 0, 2)).reshape(4, pixels)
    proj = [own] + [swap(own, "dev", members, 2 * s) for s in range(1, chunks)]
    part0 = jnp.transpose(particles, (1, 0, 2)).reshape(2 * n, pixels)
    ints0 = jnp.concatenate([defocus_bin[:, None], candidates], axis=1)
    part1 = swap(part0, "dev", members, 1)
    ints1 = swap(ints0, "dev", members, 1)

    prep = call(
        prep_kernel,
        jax.ShapeDtypeStruct((6 * n, pixels), bf16),
        flops=10 * n * pixels,
        moved=16 * n * pixels,
    )
    y0 = prep(part0, ints0, ctf_table, trig)
    y1 = prep(part1, ints1, ctf_table, trig)

    lane = jnp.arange(rows, dtype=jnp.int32) % wide
    pid = 4 * ((dev // 2) ^ (lane // 4)) + 2 * (dev % 2) + lane % 2
    m0, m1, share, stat = call(
        functools.partial(score_kernel, chunks, rows),
        (
            jax.ShapeDtypeStruct((6 * n, rows), f32),
            jax.ShapeDtypeStruct((6 * n, rows), f32),
            jax.ShapeDtypeStruct((2 * n, rows), f32),
            jax.ShapeDtypeStruct((2 * n, LINE_LEN), f32),
        ),
        scratch_shapes=[pltpu.VMEM((rows, pixels), bf16), pltpu.VMEM((2 * bins, pixels), bf16)],
        flops=2 * 224 * rows * pixels,
        moved=30 * n * pixels,
    )(*proj, y0, y1, ints0, ints1, ctf_table, noise, trig, pid[None, :])
    other = swap(stat, "dev", members, 1)
    sums = call(
        functools.partial(slice_kernel, chunks),
        tuple(jax.ShapeDtypeStruct((4, pixels + LINE_LEN), bf16) for _ in range(chunks)),
        flops=2 * 192 * 3 * wide * pixels,
        moved=30 * n * pixels,
    )(y0, y1, m0, m1, share, stat, other, ints0, ints1, trig)
    parts = [sums[0]] + [swap(sums[s], "dev", members, 2 * s) for s in range(1, chunks)]

    group_ids = jnp.arange(groups, dtype=jnp.int32)
    slab_hit = line_slab[:, :, None] == group_ids[None, None, :]
    owner_line = jnp.sum(jnp.where(slab_hit, slab_owner[None, None, :], 0), axis=2)
    line_ids = jnp.arange(lines, dtype=jnp.int32)
    earlier = line_ids[None, :] < line_ids[:, None]
    same_owner = owner_line[:, :, None] == owner_line[:, None, :]
    line_rank = jnp.sum(jnp.logical_and(same_owner, earlier[None]), axis=2)
    rel = owner_line ^ grp
    place = jnp.zeros_like(rel)
    bits = groups.bit_length() - 1
    for b in range(bits):
        place = place + (((rel >> b) & 1) << (bits - 1 - b))
    idx = (4 * cap) * place + 2 * cap * jnp.arange(2, dtype=jnp.int32)[:, None] + line_rank
    idx = idx.astype(jnp.int32)

    sel = call(
        functools.partial(table_kernel, lines, cap),
        jax.ShapeDtypeStruct((2, cap, bins, LINE_LEN), f32),
        in_specs=[pl.BlockSpec(memory_space=pltpu.SMEM), pl.BlockSpec(memory_space=pltpu.VMEM)],
        flops=bins * pixels,
        moved=4 * bins * pixels,
    )(idx, ctf_table)
    half = groups // 2 * 4 * cap
    keep, send = call(
        functools.partial(pack_kernel, chunks, lines, cap),
        (
            jax.ShapeDtypeStruct((half + 16, LINE_LEN), f32),
            jax.ShapeDtypeStruct((half + 16, LINE_LEN), bf16),
        ),
        in_specs=[pl.BlockSpec(memory_space=pltpu.SMEM)]
        + [pl.BlockSpec(memory_space=pltpu.VMEM)] * chunks,
        scratch_shapes=[pltpu.VMEM((2 * half, LINE_LEN), f32)],
        flops=16 * pixels,
        moved=64 * pixels,
    )(idx, *parts)
    for b in range(bits - 1):
        total = keep + swap(send, "grp", groups, 1 << b).astype(f32)
        keep, send, tail = total[: half // 2], total[half // 2 : half], total[half:]
        half = half // 2
        send = jnp.concatenate([send, tail], axis=0).astype(bf16)
        if b < bits - 2:
            keep = jnp.concatenate([keep, tail], axis=0)
    recv = swap(send, "grp", groups, 1 << (bits - 1))
    weight_scale = 2 * members / (n * groups * members)
    return call(
        functools.partial(final_kernel, cap, weight_scale),
        (
            jax.ShapeDtypeStruct((1, 2, 2, cap, LINE_LEN), f32),
            jax.ShapeDtypeStruct((1, 2, cap, LINE_LEN), f32),
        ),
        flops=1000,
        moved=8 * 4 * cap * LINE_LEN,
    )(keep, recv, tail, sel)


def solution(mesh):
    return jax.shard_map(
        body,
        mesh=mesh,
        in_specs=(
            P(("grp", "dev"), None, None),
            P(("grp", "dev")),
            P(("grp", "dev"), None),
            P("dev", None, None),
            P(),
            P(),
            P("dev", None),
            P(),
        ),
        out_specs=(P("grp", "dev", None, None, None), P("grp", "dev", None, None)),
        check_vma=False,
    )
```

```python
import functools
import math

import jax
import jax.numpy as jnp
import numpy as np
from jax import lax
from jax.experimental import pallas as pl
from jax.experimental.pallas import tpu as pltpu
from jax.sharding import PartitionSpec as P

LINE_LEN = 128
STEP = 2.0 * math.pi / LINE_LEN
VMEM_BYTES = 40 * 1024 * 1024
f32 = jnp.float32
bf16 = jnp.bfloat16
exact = lax.Precision.HIGHEST
last_last = (((1,), (1,)), ((), ()))
first_first = (((0,), (0,)), ((), ()))


def trig_rows():
    column = np.arange(LINE_LEN)
    freq = np.where(column < LINE_LEN // 2, column, column - LINE_LEN)
    rows = np.zeros((8, LINE_LEN), np.float32)
    rows[0] = np.cos(freq * STEP)
    rows[1] = np.sin(freq * STEP)
    return rows


def far_first(count):
    return reversed(range(1, count))


def call(kernel, out_shape, flops=0, moved=0, **kw):
    return pl.pallas_call(
        kernel,
        out_shape=out_shape,
        compiler_params=pltpu.CompilerParams(vmem_limit_bytes=VMEM_BYTES),
        cost_estimate=pl.CostEstimate(flops=flops, bytes_accessed=moved, transcendentals=0),
        **kw,
    )


def spread(first, second):
    rows, n = first.shape
    rest = jnp.full((rows, LINE_LEN - 2 * n), -1, jnp.int32)
    return jnp.concatenate([first, second, rest], axis=1)


def onehot_of(d0_ref, d1_ref, bins):
    row = spread(d0_ref[...], d1_ref[...])
    return (row == lax.broadcasted_iota(jnp.int32, (bins, LINE_LEN), 0)).astype(f32)


def prep_half(h, part, defocus, tab_ref, y_ref, scr_ref, ctf_ref):
    n = defocus.shape[1]
    bins, pixels = tab_ref.shape
    lines = pixels // LINE_LEN
    onehot = (defocus == lax.broadcasted_iota(jnp.int32, (bins, n), 0)).astype(f32)
    scr_ref[...] = part.astype(f32)
    ctf_ref[...] = lax.dot_general(
        onehot.astype(bf16), tab_ref[...], first_first, preferred_element_type=f32
    )
    for l in range(lines):
        cols = slice(l * LINE_LEN, (l + 1) * LINE_LEN)
        ctf = ctf_ref[:, cols]
        for part in range(2):
            x = scr_ref[pl.ds(2 * l + part, n, stride=2 * lines), :] * ctf
            base = (2 * part + h) * n
            y_ref[base : base + n, cols] = x.astype(bf16)
            base += 4 * n
            y_ref[base : base + n, cols] = (x * math.cos(l * STEP)).astype(bf16)
            base += 4 * n
            y_ref[base : base + n, cols] = (x * math.sin(l * STEP)).astype(bf16)


def own_kernel(p_hbm, t_hbm, d_hbm, y_ref, tab_ref, raw_ref, d_ref, scr_ref, ctf_ref, sems):
    copies = [
        pltpu.make_async_copy(src, dst, sems.at[i])
        for i, (src, dst) in enumerate(((t_hbm, tab_ref), (p_hbm, raw_ref), (d_hbm, d_ref)))
    ]
    for copy in copies:
        copy.start()
    for copy in copies:
        copy.wait()
    prep_half(0, raw_ref[...], d_ref[...], tab_ref, y_ref, scr_ref, ctf_ref)


def partner_kernel(p_ref, tab_ref, d_ref, half_ref, y_ref, scr_ref, ctf_ref):
    prep_half(1, p_ref[...], d_ref[...], tab_ref, y_ref, scr_ref, ctf_ref)


def score_kernel(chunks, *refs):
    p_refs = refs[:chunks]
    y_ref, tab_ref, d0_ref, d1_ref, c0_ref, c1_ref, noise_ref, trig_ref, pid_ref = refs[
        chunks : chunks + 9
    ]
    m_ref, s_ref, stat_ref = refs[chunks + 9 : chunks + 12]
    scr_ref, r_ref, g_ref = refs[chunks + 12 :]
    n = d0_ref.shape[1]
    bins, pixels = tab_ref.shape
    lines = pixels // LINE_LEN
    half = 2 * chunks
    wide = 2 * half
    size = 4 * lines
    for s, p in enumerate(p_refs):
        scr_ref[s * size : (s + 1) * size] = p[...].astype(f32)
    cos_row, sin_row = trig_ref[0:1], trig_ref[1:2]
    power = [None] * half
    for l in range(lines):
        cols = slice(l * LINE_LEN, (l + 1) * LINE_LEN)
        x = jnp.concatenate(
            [scr_ref[pl.ds(2 * l + part, half, stride=2 * lines), :] for part in range(2)], axis=0
        )
        one = x * noise_ref[:, cols]
        r_ref[0:wide, cols] = one.astype(bf16)
        r_ref[wide : 2 * wide, cols] = (one * cos_row).astype(bf16)
        r_ref[2 * wide : 3 * wide, cols] = (one * sin_row).astype(bf16)
        square = one * x
        square = square[:half] + square[half:]
        t = tab_ref[:, cols].astype(f32)
        t = t * t
        for j in range(half):
            term = t * square[j : j + 1]
            power[j] = term if l == 0 else power[j] + term
    g_ref[:, : y_ref.shape[0]] = lax.dot_general(
        r_ref[...], y_ref[...], last_last, preferred_element_type=f32
    )
    step = 2 * n

    def left(v, k):
        return pltpu.roll(v, LINE_LEN - k, 1) if k else v

    def right(v, k):
        return pltpu.roll(v, k, 1) if k else v

    def block(k):
        at = k * step // LINE_LEN * LINE_LEN
        return left(g_ref[: 3 * wide, at : at + LINE_LEN], k * step - at)

    even, odd = [], []
    for a in range(3):
        real, imag = block(2 * a), block(2 * a + 1)
        row = [(v * wide, v * wide + half, (v + 1) * wide) for v in range(3)]
        even.append([real[i:j] + imag[j:k] for i, j, k in row])
        odd.append([imag[i:j] - real[j:k] for i, j, k in row])
    onehot = onehot_of(d0_ref, d1_ref, bins)
    quad = 0.5 * jnp.concatenate(
        [
            jnp.sum(onehot * jnp.sum(p, axis=1, keepdims=True), axis=0, keepdims=True)
            for p in power
        ],
        axis=0,
    )
    pid = pid_ref[...]
    cand = spread(c0_ref[...], c1_ref[...])
    listed = cand[0:1] == pid
    for c in range(1, cand.shape[0]):
        listed = jnp.logical_or(listed, cand[c : c + 1] == pid)

    scores = []
    for a, sign in ((0, 0), (1, 1), (1, -1)):
        still, base, turn = even[a][0], even[a][1], odd[a][2]
        if sign == 1:
            still, base, turn = still + odd[2][0], base + odd[2][1], turn - even[2][2]
        if sign == -1:
            still, base, turn = still - odd[2][0], base - odd[2][1], turn + even[2][2]
        still, base = still - quad, base - quad
        scores.append([jnp.where(listed, v, -3.0e38) for v in (still, base + turn, base - turn)])
    peak = scores[0][0]
    for v in scores[0][1:] + scores[1] + scores[2]:
        peak = jnp.maximum(peak, v)
    peak = jnp.max(peak, axis=0, keepdims=True)
    terms = [[jnp.where(listed, jnp.exp(v - peak), 0.0) for v in group] for group in scores]
    both = [p + m for _, p, m in terms]
    diff = [p - m for _, p, m in terms]
    still = [s for s, _, _ in terms]
    total = (still[0] + both[0]) + (still[1] + both[1]) + (still[2] + both[2])
    s_ref[...] = total
    mass = jnp.sum(total, axis=0, keepdims=True)
    stat_ref[...] = jnp.concatenate([peak, mass, jnp.zeros((6, LINE_LEN), f32)], axis=0)
    alpha = [
        [still[0], both[0], None],
        [still[1] + still[2], both[1] + both[2], None],
        [None, None, diff[2] - diff[1]],
    ]
    beta = [
        [None, None, diff[0]],
        [None, None, diff[1] + diff[2]],
        [still[1] - still[2], both[1] - both[2], None],
    ]
    zero = jnp.zeros((half, LINE_LEN), f32)
    for b in range(3):
        for at in range(0, 2 * LINE_LEN, LINE_LEN):
            real, imag = zero, zero
            for a in range(3):
                for part in range(2):
                    k = (2 * a + part) * step - at
                    if not 0 <= k < LINE_LEN:
                        continue
                    if alpha[a][b] is not None:
                        if part == 0:
                            real = real + right(alpha[a][b], k)
                        else:
                            imag = imag + right(alpha[a][b], k)
                    elif part == 0:
                        imag = imag - right(beta[a][b], k)
                    else:
                        real = real + right(beta[a][b], k)
            m_ref[b * wide : (b + 1) * wide, at : at + LINE_LEN] = by_chunk(real, imag)


def by_chunk(real, imag):
    pieces = []
    for s in range(real.shape[0] // 2):
        pieces += [real[2 * s : 2 * s + 2], imag[2 * s : 2 * s + 2]]
    return jnp.concatenate(pieces, axis=0)


def slice_kernel(
    y_ref, m_ref, s_ref, stat_ref, other_ref, d0_ref, d1_ref, trig_ref, keep_ref, *send_refs
):
    n = d0_ref.shape[1]
    pixels = y_ref.shape[1]
    half = s_ref.shape[0]
    wide = 2 * half
    lane = lax.broadcasted_iota(jnp.int32, (1, LINE_LEN), 1)
    other = other_ref[...]
    other = jnp.where(lane < n, pltpu.roll(other, LINE_LEN - n, 1), pltpu.roll(other, n, 1))
    peak0, mass0 = stat_ref[0:1], stat_ref[1:2]
    peak1, mass1 = other[0:1], other[1:2]
    peak = jnp.maximum(peak0, peak1)
    grow = jnp.exp(peak0 - peak)
    scale = grow / (mass0 * grow + mass1 * jnp.exp(peak1 - peak))
    scale = jnp.where(lane < 2 * n, scale, 0.0)
    share = lax.dot_general(
        s_ref[...] * scale,
        onehot_of(d0_ref, d1_ref, LINE_LEN),
        last_last,
        precision=exact,
        preferred_element_type=f32,
    )
    share = by_chunk(share, jnp.zeros_like(share))
    scales = scale
    for k in range(2 * n, LINE_LEN, 2 * n):
        scales = scales + pltpu.roll(scale, k, 1)
    m = m_ref[...] * jnp.concatenate([scales, scales], axis=1)
    m = m.astype(bf16)[:, : 12 * n]
    width = 1024
    cos_row = jnp.concatenate([trig_ref[0:1]] * (width // LINE_LEN), axis=1)
    sin_row = jnp.concatenate([trig_ref[1:2]] * (width // LINE_LEN), axis=1)
    for c in range(pixels // width):
        cols = slice(c * width, (c + 1) * width)
        x = jnp.dot(m, y_ref[:, cols], preferred_element_type=f32)
        x = x[:wide] + x[wide : 2 * wide] * cos_row + x[2 * wide :] * sin_row
        keep_ref[:, cols] = x[:4]
        for s, ref in enumerate(send_refs, 1):
            ref[:, cols] = x[4 * s : 4 * s + 4].astype(bf16)
    keep_ref[:, pixels:] = share[:4]
    for s, ref in enumerate(send_refs, 1):
        ref[:, pixels:] = share[4 * s : 4 * s + 4].astype(bf16)


def pack_kernel(lines, cap, groups, chunks, idx_ref, own_ref, *refs):
    recv_refs = refs[: chunks - 1]
    keep_ref, *send_refs, scr_ref = refs[chunks - 1 :]
    size = 4 * cap
    scr_ref[...] = jnp.zeros(scr_ref.shape, f32)
    for l in range(lines + 1):
        cols = slice(l * LINE_LEN, (l + 1) * LINE_LEN)
        x = own_ref[:, cols]
        for ref in recv_refs:
            x = x + ref[:, cols].astype(f32)
        if l < lines:
            for j in range(2):
                row = idx_ref[j, l]
                scr_ref[pl.ds(row, 1), :] = x[j : j + 1]
                scr_ref[pl.ds(row + cap, 1), :] = x[2 + j : 3 + j]
        else:
            tail = jnp.concatenate([x, jnp.zeros((12, LINE_LEN), f32)], axis=0)
    keep_ref[:size] = scr_ref[:size]
    keep_ref[size:] = tail
    for r, ref in enumerate(send_refs, 1):
        ref[:size] = scr_ref[r * size : (r + 1) * size].astype(bf16)
        ref[size:] = tail.astype(bf16)


def table_kernel(lines, cap, idx_ref, table_ref, sel_ref):
    bins = table_ref.shape[0]
    sel_ref[...] = jnp.zeros(sel_ref.shape, f32)
    for l in range(lines):
        t = table_ref[:, l * LINE_LEN : (l + 1) * LINE_LEN].astype(f32)
        t = t * t
        for j in range(2):
            slot = idx_ref[j, l]

            @pl.when(slot < 4 * cap)
            def _():
                sel_ref[j, pl.ds(slot - 2 * cap * j, 1)] = t[None]


def final_kernel(cap, scale, own_ref, *refs):
    *recv_refs, sel_ref, data_ref, weight_ref = refs
    x = own_ref[...]
    for ref in recv_refs:
        x = x + ref[...].astype(f32)
    data_ref[...] = x[: 4 * cap].reshape(data_ref.shape)
    bt = jnp.transpose(x[4 * cap :] * scale)[: sel_ref.shape[2]]
    for j in range(2):
        weight_ref[0, j] = jnp.sum(sel_ref[j] * bt[:, j : j + 1][None], axis=1)


def body(
    particles, defocus_bin, candidates, projections, ctf_table, inv_noise, line_slab, slab_owner
):
    n, _, pixels = particles.shape
    groups = lax.axis_size("grp")
    members = lax.axis_size("dev")
    chunks = members // 2
    chip_bits = chunks.bit_length() - 1
    lines = line_slab.shape[1]
    cap = 2 * lines // groups
    bins = ctf_table.shape[0]
    wide = 4 * chunks
    dev = lax.axis_index("dev")
    grp = lax.axis_index("grp")
    trig = jnp.asarray(trig_rows())
    noise = inv_noise[None, :]

    def swap(x, axis, size, mask):
        return lax.ppermute(x, axis, [(i, i ^ mask) for i in range(size)])

    def turned(t):
        k = chip_bits // 2
        return ((t << k) | (t >> (chip_bits - k))) & (chunks - 1)

    def to_place(x, t):
        return lax.ppermute(
            x, "dev", [(i, i ^ (2 * (turned(t) if i % 2 else t))) for i in range(members)]
        )

    def as_lines(x):
        count = x.shape[0]
        x = x.reshape(count, 2, lines, LINE_LEN)
        return jnp.transpose(x, (0, 2, 1, 3)).reshape(2 * count * lines, LINE_LEN)

    part0, part1 = as_lines(particles), as_lines(swap(particles, "dev", members, 1))
    def0, def1 = defocus_bin[None, :], swap(defocus_bin, "dev", members, 1)[None, :]
    cand0, cand1 = candidates.T, swap(candidates, "dev", members, 1).T
    proj = {t: to_place(projections, t) for t in far_first(chunks)}
    proj = [as_lines(p) for p in [projections] + [proj[t] for t in range(1, chunks)]]

    def in_hbm(x):
        return pltpu.with_memory_space_constraint(x, pltpu.HBM)

    vmem = pl.BlockSpec(memory_space=pltpu.VMEM)
    hbm = pl.BlockSpec(memory_space=pl.ANY)
    scratch = [pltpu.VMEM((2 * n * lines, LINE_LEN), f32), pltpu.VMEM((n, pixels), f32)]
    y, table = call(
        own_kernel,
        (
            jax.ShapeDtypeStruct((12 * n, pixels), bf16),
            jax.ShapeDtypeStruct((bins, pixels), bf16),
        ),
        in_specs=[hbm] * 3,
        scratch_shapes=[
            pltpu.VMEM((2 * n * lines, LINE_LEN), bf16),
            pltpu.VMEM((1, n), jnp.int32),
            *scratch,
            pltpu.SemaphoreType.DMA((3,)),
        ],
        flops=20 * n * pixels,
        moved=32 * n * pixels,
    )(in_hbm(part0), in_hbm(ctf_table), in_hbm(def0))
    y = call(
        partner_kernel,
        jax.ShapeDtypeStruct((12 * n, pixels), bf16),
        in_specs=[vmem, vmem, vmem, hbm],
        scratch_shapes=scratch,
        input_output_aliases={3: 0},
        flops=20 * n * pixels,
        moved=32 * n * pixels,
    )(part1, table, def1, y)

    row = lax.broadcasted_iota(jnp.int32, (2 * chunks, LINE_LEN), 0)
    far = jnp.where(dev % 2 == 0, row // 2, turned(row // 2))
    pid = 4 * ((dev // 2) ^ far) + 2 * (dev % 2) + row % 2
    m, share, stat = call(
        functools.partial(score_kernel, chunks),
        (
            jax.ShapeDtypeStruct((3 * wide, 2 * LINE_LEN), f32),
            jax.ShapeDtypeStruct((2 * chunks, LINE_LEN), f32),
            jax.ShapeDtypeStruct((8, LINE_LEN), f32),
        ),
        scratch_shapes=[
            pltpu.VMEM((4 * lines * chunks, LINE_LEN), f32),
            pltpu.VMEM((3 * wide, pixels), bf16),
            pltpu.VMEM((3 * wide, 2 * LINE_LEN), f32),
        ],
        flops=2 * 192 * 3 * wide * pixels,
        moved=30 * n * pixels,
    )(*proj, y, table, def0, def1, cand0, cand1, noise, trig, pid)
    line_slab, stat = lax.optimization_barrier((line_slab, stat))
    other = swap(stat, "dev", members, 1)
    own, *send = call(
        slice_kernel,
        (jax.ShapeDtypeStruct((4, pixels + LINE_LEN), f32),)
        + (jax.ShapeDtypeStruct((4, pixels + LINE_LEN), bf16),) * (chunks - 1),
        flops=2 * 192 * 3 * wide * pixels,
        moved=30 * n * pixels,
    )(y, m, share, stat, other, def0, def1, trig)
    got = [to_place(send[t - 1], t) for t in far_first(chunks)]

    group_ids = jnp.arange(groups, dtype=jnp.int32)
    slab_hit = line_slab[:, :, None] == group_ids[None, None, :]
    owner_line = jnp.sum(jnp.where(slab_hit, slab_owner[None, None, :], 0), axis=2)
    line_ids = jnp.arange(lines, dtype=jnp.int32)
    earlier = line_ids[None, :] < line_ids[:, None]
    same_owner = owner_line[:, :, None] == owner_line[:, None, :]
    line_rank = jnp.sum(jnp.logical_and(same_owner, earlier[None]), axis=2)
    rel = owner_line ^ grp
    idx = (4 * cap) * rel + 2 * cap * jnp.arange(2, dtype=jnp.int32)[:, None] + line_rank
    idx = idx.astype(jnp.int32)

    sel = call(
        functools.partial(table_kernel, lines, cap),
        jax.ShapeDtypeStruct((2, cap, bins, LINE_LEN), f32),
        in_specs=[pl.BlockSpec(memory_space=pltpu.SMEM), pl.BlockSpec(memory_space=pltpu.VMEM)],
        flops=bins * pixels,
        moved=4 * bins * pixels,
    )(idx, table)
    size = 4 * cap + 16
    keep, *send = call(
        functools.partial(pack_kernel, lines, cap, groups, chunks),
        (jax.ShapeDtypeStruct((size, LINE_LEN), f32),)
        + (jax.ShapeDtypeStruct((size, LINE_LEN), bf16),) * (groups - 1),
        in_specs=[pl.BlockSpec(memory_space=pltpu.SMEM)] + [vmem] * chunks,
        scratch_shapes=[pltpu.VMEM((4 * cap * groups, LINE_LEN), f32)],
        flops=16 * pixels,
        moved=64 * pixels,
    )(idx, own, *got)
    recv = [swap(send[r - 1], "grp", groups, r) for r in far_first(groups)]
    weight_scale = 2 * members / (n * groups * members)
    return call(
        functools.partial(final_kernel, cap, weight_scale),
        (
            jax.ShapeDtypeStruct((1, 2, 2, cap, LINE_LEN), f32),
            jax.ShapeDtypeStruct((1, 2, cap, LINE_LEN), f32),
        ),
        flops=1000,
        moved=8 * 4 * cap * LINE_LEN,
    )(keep, *recv, sel)


def solution(mesh):
    return jax.shard_map(
        body,
        mesh=mesh,
        in_specs=(
            P(("grp", "dev"), None, None),
            P(("grp", "dev")),
            P(("grp", "dev"), None),
            P("dev", None, None),
            P(),
            P(),
            P("dev", None),
            P(),
        ),
        out_specs=(P("grp", "dev", None, None, None), P("grp", "dev", None, None)),
        check_vma=False,
    )
```

```python
import functools
import math

import jax
import jax.numpy as jnp
import numpy as np
from jax import lax
from jax.experimental import pallas as pl
from jax.experimental.pallas import tpu as pltpu
from jax.sharding import PartitionSpec as P

LINE_LEN = 128
STEP = 2.0 * math.pi / LINE_LEN
VMEM_BYTES = 40 * 1024 * 1024
f32 = jnp.float32
bf16 = jnp.bfloat16
exact = lax.Precision.HIGHEST
last_last = (((1,), (1,)), ((), ()))
first_first = (((0,), (0,)), ((), ()))


def trig_rows():
    column = np.arange(LINE_LEN)
    freq = np.where(column < LINE_LEN // 2, column, column - LINE_LEN)
    rows = np.zeros((8, LINE_LEN), np.float32)
    rows[0] = np.cos(freq * STEP)
    rows[1] = np.sin(freq * STEP)
    return rows


def far_first(count):
    return list(range(count - 1, 0, -1))


def nearest_first_then_far(count):
    order = far_first(count)
    return order[-1:] + order[:-1]


def call(kernel, out_shape, flops=0, moved=0, **kw):
    return pl.pallas_call(
        kernel,
        out_shape=out_shape,
        compiler_params=pltpu.CompilerParams(vmem_limit_bytes=VMEM_BYTES),
        cost_estimate=pl.CostEstimate(flops=flops, bytes_accessed=moved, transcendentals=0),
        **kw,
    )


def spread(first, second):
    rows, n = first.shape
    rest = jnp.full((rows, LINE_LEN - 2 * n), -1, jnp.int32)
    return jnp.concatenate([first, second, rest], axis=1)


def onehot_of(i0_ref, i1_ref, bins):
    row = spread(i0_ref[8:9], i1_ref[8:9])
    return (row == lax.broadcasted_iota(jnp.int32, (bins, LINE_LEN), 0)).astype(f32)


def prep_half(h, part, defocus, tab_ref, y_ref, scr_ref, ctf_ref):
    n = defocus.shape[1]
    bins, pixels = tab_ref.shape
    lines = pixels // LINE_LEN
    onehot = (defocus == lax.broadcasted_iota(jnp.int32, (bins, n), 0)).astype(f32)
    scr_ref[...] = part.astype(f32)
    ctf_ref[...] = lax.dot_general(
        onehot.astype(bf16), tab_ref[...], first_first, preferred_element_type=f32
    )
    for l in range(lines):
        cols = slice(l * LINE_LEN, (l + 1) * LINE_LEN)
        ctf = ctf_ref[:, cols]
        for part in range(2):
            x = scr_ref[pl.ds(2 * l + part, n, stride=2 * lines), :] * ctf
            base = (2 * part + h) * n
            y_ref[base : base + n, cols] = x.astype(bf16)
            base += 4 * n
            y_ref[base : base + n, cols] = (x * math.cos(l * STEP)).astype(bf16)
            base += 4 * n
            y_ref[base : base + n, cols] = (x * math.sin(l * STEP)).astype(bf16)


def load_kernel(p_hbm, t_hbm, c_hbm, d_hbm, raw_ref, tab_ref, ints_ref, c_ref, d_ref, sems):
    copies = [
        pltpu.make_async_copy(src, dst, sems.at[i])
        for i, (src, dst) in enumerate(
            ((p_hbm, raw_ref), (t_hbm, tab_ref), (c_hbm, c_ref), (d_hbm, d_ref))
        )
    ]
    for copy in copies:
        copy.start()
    for copy in copies:
        copy.wait()
    ints_ref[0:8] = c_ref[...]
    ints_ref[8:] = jnp.broadcast_to(d_ref[...], (8, d_ref.shape[1]))


def own_kernel(p_ref, tab_ref, d_ref, y_ref, scr_ref, ctf_ref):
    prep_half(0, p_ref[...], d_ref[8:9], tab_ref, y_ref, scr_ref, ctf_ref)


def partner_kernel(p_ref, tab_ref, d_ref, half_ref, y_ref, scr_ref, ctf_ref):
    prep_half(1, p_ref[...], d_ref[8:9], tab_ref, y_ref, scr_ref, ctf_ref)


def score_kernel(chunks, *refs):
    p_refs = refs[:chunks]
    y_ref, tab_ref, i0_ref, i1_ref, noise_ref, trig_ref, pid_ref = refs[chunks : chunks + 7]
    m_ref, s_ref, stat_ref = refs[chunks + 7 : chunks + 10]
    scr_ref, r_ref, g_ref = refs[chunks + 10 :]
    n = i0_ref.shape[1]
    bins, pixels = tab_ref.shape
    lines = pixels // LINE_LEN
    half = 2 * chunks
    wide = 2 * half
    size = 4 * lines
    for s, p in enumerate(p_refs):
        scr_ref[s * size : (s + 1) * size] = p[...].astype(f32)
    cos_row, sin_row = trig_ref[0:1], trig_ref[1:2]
    power = [None] * half
    for l in range(lines):
        cols = slice(l * LINE_LEN, (l + 1) * LINE_LEN)
        x = jnp.concatenate(
            [scr_ref[pl.ds(2 * l + part, half, stride=2 * lines), :] for part in range(2)], axis=0
        )
        one = x * noise_ref[:, cols]
        r_ref[0:wide, cols] = one.astype(bf16)
        r_ref[wide : 2 * wide, cols] = (one * cos_row).astype(bf16)
        r_ref[2 * wide : 3 * wide, cols] = (one * sin_row).astype(bf16)
        square = one * x
        square = square[:half] + square[half:]
        t = tab_ref[:, cols].astype(f32)
        t = t * t
        for j in range(half):
            term = t * square[j : j + 1]
            power[j] = term if l == 0 else power[j] + term
    g_ref[:, : y_ref.shape[0]] = lax.dot_general(
        r_ref[...], y_ref[...], last_last, preferred_element_type=f32
    )
    step = 2 * n

    def left(v, k):
        return pltpu.roll(v, LINE_LEN - k, 1) if k else v

    def right(v, k):
        return pltpu.roll(v, k, 1) if k else v

    def block(k):
        at = k * step // LINE_LEN * LINE_LEN
        return left(g_ref[: 3 * wide, at : at + LINE_LEN], k * step - at)

    even, odd = [], []
    for a in range(3):
        real, imag = block(2 * a), block(2 * a + 1)
        row = [(v * wide, v * wide + half, (v + 1) * wide) for v in range(3)]
        even.append([real[i:j] + imag[j:k] for i, j, k in row])
        odd.append([imag[i:j] - real[j:k] for i, j, k in row])
    onehot = onehot_of(i0_ref, i1_ref, bins)
    quad = 0.5 * jnp.concatenate(
        [
            jnp.sum(onehot * jnp.sum(p, axis=1, keepdims=True), axis=0, keepdims=True)
            for p in power
        ],
        axis=0,
    )
    pid = pid_ref[...]
    cand = spread(i0_ref[0:8], i1_ref[0:8])
    listed = cand[0:1] == pid
    for c in range(1, cand.shape[0]):
        listed = jnp.logical_or(listed, cand[c : c + 1] == pid)

    scores = []
    for a, sign in ((0, 0), (1, 1), (1, -1)):
        still, base, turn = even[a][0], even[a][1], odd[a][2]
        if sign == 1:
            still, base, turn = still + odd[2][0], base + odd[2][1], turn - even[2][2]
        if sign == -1:
            still, base, turn = still - odd[2][0], base - odd[2][1], turn + even[2][2]
        still, base = still - quad, base - quad
        scores.append([jnp.where(listed, v, -3.0e38) for v in (still, base + turn, base - turn)])
    peak = scores[0][0]
    for v in scores[0][1:] + scores[1] + scores[2]:
        peak = jnp.maximum(peak, v)
    peak = jnp.max(peak, axis=0, keepdims=True)
    terms = [[jnp.where(listed, jnp.exp(v - peak), 0.0) for v in group] for group in scores]
    both = [p + m for _, p, m in terms]
    diff = [p - m for _, p, m in terms]
    still = [s for s, _, _ in terms]
    total = (still[0] + both[0]) + (still[1] + both[1]) + (still[2] + both[2])
    s_ref[...] = total
    mass = jnp.sum(total, axis=0, keepdims=True)
    stat_ref[...] = jnp.concatenate([peak, mass, jnp.zeros((6, LINE_LEN), f32)], axis=0)
    alpha = [
        [still[0], both[0], None],
        [still[1] + still[2], both[1] + both[2], None],
        [None, None, diff[2] - diff[1]],
    ]
    beta = [
        [None, None, diff[0]],
        [None, None, diff[1] + diff[2]],
        [still[1] - still[2], both[1] - both[2], None],
    ]
    zero = jnp.zeros((half, LINE_LEN), f32)
    for b in range(3):
        for at in range(0, 2 * LINE_LEN, LINE_LEN):
            real, imag = zero, zero
            for a in range(3):
                for part in range(2):
                    k = (2 * a + part) * step - at
                    if not 0 <= k < LINE_LEN:
                        continue
                    if alpha[a][b] is not None:
                        if part == 0:
                            real = real + right(alpha[a][b], k)
                        else:
                            imag = imag + right(alpha[a][b], k)
                    elif part == 0:
                        imag = imag - right(beta[a][b], k)
                    else:
                        real = real + right(beta[a][b], k)
            m_ref[b * wide : (b + 1) * wide, at : at + LINE_LEN] = by_chunk(real, imag)


def by_chunk(real, imag):
    pieces = []
    for s in range(real.shape[0] // 2):
        pieces += [real[2 * s : 2 * s + 2], imag[2 * s : 2 * s + 2]]
    return jnp.concatenate(pieces, axis=0)


def slice_kernel(
    y_ref, m_ref, s_ref, stat_ref, other_ref, i0_ref, i1_ref, trig_ref, keep_ref, *send_refs
):
    n = i0_ref.shape[1]
    pixels = y_ref.shape[1]
    half = s_ref.shape[0]
    wide = 2 * half
    lane = lax.broadcasted_iota(jnp.int32, (1, LINE_LEN), 1)
    other = other_ref[...]
    other = jnp.where(lane < n, pltpu.roll(other, LINE_LEN - n, 1), pltpu.roll(other, n, 1))
    peak0, mass0 = stat_ref[0:1], stat_ref[1:2]
    peak1, mass1 = other[0:1], other[1:2]
    peak = jnp.maximum(peak0, peak1)
    grow = jnp.exp(peak0 - peak)
    scale = grow / (mass0 * grow + mass1 * jnp.exp(peak1 - peak))
    scale = jnp.where(lane < 2 * n, scale, 0.0)
    share = lax.dot_general(
        s_ref[...] * scale,
        onehot_of(i0_ref, i1_ref, LINE_LEN),
        last_last,
        precision=exact,
        preferred_element_type=f32,
    )
    share = by_chunk(share, jnp.zeros_like(share))
    scales = scale
    for k in range(2 * n, LINE_LEN, 2 * n):
        scales = scales + pltpu.roll(scale, k, 1)
    m = m_ref[...] * jnp.concatenate([scales, scales], axis=1)
    m = m.astype(bf16)[:, : 12 * n]
    width = 1024
    cos_row = jnp.concatenate([trig_ref[0:1]] * (width // LINE_LEN), axis=1)
    sin_row = jnp.concatenate([trig_ref[1:2]] * (width // LINE_LEN), axis=1)
    for c in range(pixels // width):
        cols = slice(c * width, (c + 1) * width)
        x = jnp.dot(m, y_ref[:, cols], preferred_element_type=f32)
        x = x[:wide] + x[wide : 2 * wide] * cos_row + x[2 * wide :] * sin_row
        keep_ref[:, cols] = x[:4]
        for s, ref in enumerate(send_refs, 1):
            ref[:, cols] = x[4 * s : 4 * s + 4].astype(bf16)
    keep_ref[:, pixels:] = share[:4]
    for s, ref in enumerate(send_refs, 1):
        ref[:, pixels:] = share[4 * s : 4 * s + 4].astype(bf16)


def pack_kernel(lines, cap, chunks, slot_ref, own_ref, *refs):
    recv_refs = refs[: chunks - 1]
    keep_ref, *send_refs, scr_ref = refs[chunks - 1 :]
    size = 2 * cap
    for l in range(lines + 1):
        cols = slice(l * LINE_LEN, (l + 1) * LINE_LEN)
        x = own_ref[:, cols]
        for ref in recv_refs:
            x = x + ref[:, cols].astype(f32)
        if l < lines:
            for j in range(2):
                row = j * lines + l
                scr_ref[row : row + 1, :LINE_LEN] = x[j : j + 1]
                scr_ref[row : row + 1, LINE_LEN:] = x[2 + j : 3 + j]
        else:
            tail = jnp.concatenate([x, jnp.zeros((4, LINE_LEN), f32)], axis=0)
    slots = jnp.concatenate([slot_ref[0:1], slot_ref[1:2]], axis=1)
    rows = size * (len(send_refs) + 1)
    pick = slots == lax.broadcasted_iota(jnp.int32, (rows, 2 * lines), 0)
    packed = jnp.dot(
        pick.astype(f32).astype(bf16), scr_ref[...].astype(bf16), preferred_element_type=f32
    )
    for r, ref in enumerate([keep_ref] + send_refs):
        for part in range(2):
            piece = packed[r * size : (r + 1) * size, part * LINE_LEN : (part + 1) * LINE_LEN]
            ref[part * size : (part + 1) * size] = piece.astype(ref.dtype)
        ref[2 * size :] = tail.astype(ref.dtype)


def table_kernel(lines, cap, slot_ref, table_ref, sel_ref):
    bins = table_ref.shape[0]
    sel_ref[...] = jnp.zeros(sel_ref.shape, f32)
    for l in range(lines):
        t = table_ref[:, l * LINE_LEN : (l + 1) * LINE_LEN].astype(f32)
        t = t * t
        for j in range(2):
            slot = slot_ref[j, l]

            @pl.when(slot < 2 * cap)
            def _():
                sel_ref[j, pl.ds(slot - cap * j, bins, stride=cap), :] = t


def final_kernel(cap, bins, scale, own_ref, *refs):
    *recv_refs, sel_ref, data_hbm, weight_hbm, data_ref, weight_ref, sems = refs
    x = own_ref[...]
    for ref in recv_refs:
        x = x + ref[...].astype(f32)
    for part in range(2):
        for j in range(2):
            row = (2 * part + j) * cap
            data_ref[0, j, part] = x[row : row + cap]
    data_copy = pltpu.make_async_copy(data_ref, data_hbm, sems.at[0])
    data_copy.start()
    tail = x[4 * cap :] * scale
    for j in range(2):
        total = None
        for b in range(bins):
            term = sel_ref[j, b * cap : (b + 1) * cap] * tail[j : j + 1, b : b + 1]
            total = term if b == 0 else total + term
        weight_ref[0, j] = total
    weight_copy = pltpu.make_async_copy(weight_ref, weight_hbm, sems.at[1])
    weight_copy.start()
    data_copy.wait()
    weight_copy.wait()


def body(
    particles, defocus_bin, candidates, projections, ctf_table, inv_noise, line_slab, slab_owner
):
    n, _, pixels = particles.shape
    groups = lax.axis_size("grp")
    members = lax.axis_size("dev")
    chunks = members // 2
    chip_bits = chunks.bit_length() - 1
    lines = line_slab.shape[1]
    cap = 2 * lines // groups
    bins = ctf_table.shape[0]
    wide = 4 * chunks
    dev = lax.axis_index("dev")
    grp = lax.axis_index("grp")
    trig = jnp.asarray(trig_rows())
    noise = inv_noise[None, :]

    def swap(x, axis, size, mask):
        return lax.ppermute(x, axis, [(i, i ^ mask) for i in range(size)])

    def turned(t):
        k = chip_bits // 2
        return ((t << k) | (t >> (chip_bits - k))) & (chunks - 1)

    def to_place(x, t):
        return lax.ppermute(
            x, "dev", [(i, i ^ (2 * (turned(t) if i % 2 else t))) for i in range(members)]
        )

    def as_lines(x):
        count = x.shape[0]
        x = x.reshape(count, 2, lines, LINE_LEN)
        return jnp.transpose(x, (0, 2, 1, 3)).reshape(2 * count * lines, LINE_LEN)

    part0, part1 = as_lines(particles), as_lines(swap(particles, "dev", members, 1))
    proj = {t: to_place(projections, t) for t in far_first(chunks)}
    proj = [as_lines(p) for p in [projections] + [proj[t] for t in range(1, chunks)]]

    def in_hbm(x):
        return pltpu.with_memory_space_constraint(x, pltpu.HBM)

    vmem = pl.BlockSpec(memory_space=pltpu.VMEM)
    hbm = pl.BlockSpec(memory_space=pl.ANY)
    scratch = [pltpu.VMEM((2 * n * lines, LINE_LEN), f32), pltpu.VMEM((n, pixels), f32)]
    raw, table, ints0 = call(
        load_kernel,
        (
            jax.ShapeDtypeStruct(part0.shape, bf16),
            jax.ShapeDtypeStruct((bins, pixels), bf16),
            jax.ShapeDtypeStruct((16, n), jnp.int32),
        ),
        in_specs=[hbm] * 4,
        scratch_shapes=[
            pltpu.VMEM((8, n), jnp.int32),
            pltpu.VMEM((1, n), jnp.int32),
            pltpu.SemaphoreType.DMA((4,)),
        ],
        moved=32 * n * pixels,
    )(in_hbm(part0), in_hbm(ctf_table), in_hbm(candidates.T), in_hbm(defocus_bin[None, :]))
    ints1 = swap(ints0, "dev", members, 1)
    y = call(
        own_kernel,
        jax.ShapeDtypeStruct((12 * n, pixels), bf16),
        scratch_shapes=scratch,
        flops=20 * n * pixels,
        moved=32 * n * pixels,
    )(raw, table, ints0)
    y = call(
        partner_kernel,
        jax.ShapeDtypeStruct((12 * n, pixels), bf16),
        in_specs=[vmem, vmem, vmem, hbm],
        scratch_shapes=scratch,
        input_output_aliases={3: 0},
        flops=20 * n * pixels,
        moved=32 * n * pixels,
    )(part1, table, ints1, y)

    row = lax.broadcasted_iota(jnp.int32, (2 * chunks, LINE_LEN), 0)
    far = jnp.where(dev % 2 == 0, row // 2, turned(row // 2))
    pid = 4 * ((dev // 2) ^ far) + 2 * (dev % 2) + row % 2
    m, share, stat = call(
        functools.partial(score_kernel, chunks),
        (
            jax.ShapeDtypeStruct((3 * wide, 2 * LINE_LEN), f32),
            jax.ShapeDtypeStruct((2 * chunks, LINE_LEN), f32),
            jax.ShapeDtypeStruct((8, LINE_LEN), f32),
        ),
        scratch_shapes=[
            pltpu.VMEM((4 * lines * chunks, LINE_LEN), f32),
            pltpu.VMEM((3 * wide, pixels), bf16),
            pltpu.VMEM((3 * wide, 2 * LINE_LEN), f32),
        ],
        flops=2 * 192 * 3 * wide * pixels,
        moved=30 * n * pixels,
    )(*proj, y, table, ints0, ints1, noise, trig, pid)
    line_slab, stat = lax.optimization_barrier((line_slab, stat))
    other = swap(stat, "dev", members, 1)
    own, *send = call(
        slice_kernel,
        (jax.ShapeDtypeStruct((4, pixels + LINE_LEN), f32),)
        + (jax.ShapeDtypeStruct((4, pixels + LINE_LEN), bf16),) * (chunks - 1),
        flops=2 * 192 * 3 * wide * pixels,
        moved=30 * n * pixels,
    )(y, m, share, stat, other, ints0, ints1, trig)
    got = [to_place(send[t - 1], t) for t in far_first(chunks)]

    group_ids = jnp.arange(groups, dtype=jnp.int32)
    slab_hit = line_slab[:, :, None] == group_ids[None, None, :]
    owner_line = jnp.sum(jnp.where(slab_hit, slab_owner[None, None, :], 0), axis=2)
    line_ids = jnp.arange(lines, dtype=jnp.int32)
    earlier = line_ids[None, :] < line_ids[:, None]
    same_owner = owner_line[:, :, None] == owner_line[:, None, :]
    line_rank = jnp.sum(jnp.logical_and(same_owner, earlier[None]), axis=2)
    rel = owner_line ^ grp
    slot = (2 * cap) * rel + cap * jnp.arange(2, dtype=jnp.int32)[:, None] + line_rank
    slot = slot.astype(jnp.int32)

    sel = call(
        functools.partial(table_kernel, lines, cap),
        jax.ShapeDtypeStruct((2, bins * cap, LINE_LEN), f32),
        in_specs=[pl.BlockSpec(memory_space=pltpu.SMEM), vmem],
        flops=bins * pixels,
        moved=4 * bins * pixels,
    )(slot, table)
    size = 4 * cap + 8
    keep, *send = call(
        functools.partial(pack_kernel, lines, cap, chunks),
        (jax.ShapeDtypeStruct((size, LINE_LEN), f32),)
        + (jax.ShapeDtypeStruct((size, LINE_LEN), bf16),) * (groups - 1),
        scratch_shapes=[pltpu.VMEM((2 * lines, 2 * LINE_LEN), f32)],
        flops=16 * pixels,
        moved=64 * pixels,
    )(slot, own, *got)
    recv = [swap(send[r - 1], "grp", groups, r) for r in nearest_first_then_far(groups)]
    weight_scale = 2 * members / (n * groups * members)
    data, weight = (1, 2, 2, cap, LINE_LEN), (1, 2, cap, LINE_LEN)
    return call(
        functools.partial(final_kernel, cap, bins, weight_scale),
        (jax.ShapeDtypeStruct(data, f32), jax.ShapeDtypeStruct(weight, f32)),
        in_specs=[vmem] * (groups + 1),
        out_specs=(hbm, hbm),
        scratch_shapes=[
            pltpu.VMEM(data, f32),
            pltpu.VMEM(weight, f32),
            pltpu.SemaphoreType.DMA((2,)),
        ],
        flops=1000,
        moved=8 * 4 * cap * LINE_LEN,
    )(keep, *recv, sel)


def solution(mesh):
    return jax.shard_map(
        body,
        mesh=mesh,
        in_specs=(
            P(("grp", "dev"), None, None),
            P(("grp", "dev")),
            P(("grp", "dev"), None),
            P("dev", None, None),
            P(),
            P(),
            P("dev", None),
            P(),
        ),
        out_specs=(P("grp", "dev", None, None, None), P("grp", "dev", None, None)),
        check_vma=False,
    )
```

```python
import functools
import math

import jax
import jax.numpy as jnp
import numpy as np
from jax import lax
from jax.experimental import pallas as pl
from jax.experimental.pallas import tpu as pltpu
from jax.sharding import PartitionSpec as P

LINE_LEN = 128
STEP = 2.0 * math.pi / LINE_LEN
VMEM_BYTES = 40 * 1024 * 1024
f32 = jnp.float32
bf16 = jnp.bfloat16
exact = lax.Precision.HIGHEST
last_last = (((1,), (1,)), ((), ()))
first_first = (((0,), (0,)), ((), ()))


def trig_rows():
    column = np.arange(LINE_LEN)
    freq = np.where(column < LINE_LEN // 2, column, column - LINE_LEN)
    rows = np.zeros((8, LINE_LEN), np.float32)
    rows[0] = np.cos(freq * STEP)
    rows[1] = np.sin(freq * STEP)
    return rows


CHIP_ROUTES = [[[3, 2, 1, 0], [2, 3, 0, 1], [1, 0, 3, 2]], [[3, 2, 1, 0], [1, 3, 0, 2], [2, 0, 3, 1]]]
GROUP_ROUTES = [[[2, 3, 1, 0], [3, 2, 0, 1], [1, 0, 3, 2]], [[2, 3, 1, 0], [3, 2, 0, 1], [1, 0, 3, 2]]]


def routes(count, chosen):
    if count == 4:
        return chosen
    return [[[i ^ t for i in range(count)] for t in range(count - 1, 0, -1)]] * 2


def lookup(index, table):
    found = table[0]
    for i in range(1, len(table)):
        found = jnp.where(index == i, table[i], found)
    return found


def call(kernel, out_shape, flops=0, moved=0, **kw):
    return pl.pallas_call(
        kernel,
        out_shape=out_shape,
        compiler_params=pltpu.CompilerParams(vmem_limit_bytes=VMEM_BYTES),
        cost_estimate=pl.CostEstimate(flops=flops, bytes_accessed=moved, transcendentals=0),
        **kw,
    )


def spread(first, second):
    rows, n = first.shape
    rest = jnp.full((rows, LINE_LEN - 2 * n), -1, jnp.int32)
    return jnp.concatenate([first, second, rest], axis=1)


def onehot_of(i0_ref, i1_ref, bins):
    row = spread(i0_ref[8:9], i1_ref[8:9])
    return (row == lax.broadcasted_iota(jnp.int32, (bins, LINE_LEN), 0)).astype(f32)


def prep_half(h, part, defocus, tab_ref, y_ref, scr_ref, ctf_ref):
    n = defocus.shape[1]
    bins, pixels = tab_ref.shape
    lines = pixels // LINE_LEN
    onehot = (defocus == lax.broadcasted_iota(jnp.int32, (bins, n), 0)).astype(f32)
    scr_ref[...] = part.astype(f32)
    ctf_ref[...] = lax.dot_general(
        onehot.astype(bf16), tab_ref[...], first_first, preferred_element_type=f32
    )
    for l in range(lines):
        cols = slice(l * LINE_LEN, (l + 1) * LINE_LEN)
        ctf = ctf_ref[:, cols]
        for part in range(2):
            x = scr_ref[pl.ds(2 * l + part, n, stride=2 * lines), :] * ctf
            base = (2 * part + h) * n
            y_ref[base : base + n, cols] = x.astype(bf16)
            base += 4 * n
            y_ref[base : base + n, cols] = (x * math.cos(l * STEP)).astype(bf16)
            base += 4 * n
            y_ref[base : base + n, cols] = (x * math.sin(l * STEP)).astype(bf16)


def load_kernel(p_hbm, t_hbm, c_hbm, d_hbm, raw_ref, tab_ref, ints_ref, c_ref, d_ref, sems):
    copies = [
        pltpu.make_async_copy(src, dst, sems.at[i])
        for i, (src, dst) in enumerate(
            ((p_hbm, raw_ref), (t_hbm, tab_ref), (c_hbm, c_ref), (d_hbm, d_ref))
        )
    ]
    for copy in copies:
        copy.start()
    for copy in copies:
        copy.wait()
    ints_ref[0:8] = c_ref[...]
    ints_ref[8:] = jnp.broadcast_to(d_ref[...], (8, d_ref.shape[1]))


def own_kernel(p_ref, tab_ref, d_ref, y_ref, scr_ref, ctf_ref):
    prep_half(0, p_ref[...], d_ref[8:9], tab_ref, y_ref, scr_ref, ctf_ref)


def partner_kernel(p_ref, tab_ref, d_ref, half_ref, y_ref, scr_ref, ctf_ref):
    prep_half(1, p_ref[...], d_ref[8:9], tab_ref, y_ref, scr_ref, ctf_ref)


def score_kernel(chunks, *refs):
    p_refs = refs[:chunks]
    y_ref, tab_ref, i0_ref, i1_ref, noise_ref, trig_ref, pid_ref = refs[chunks : chunks + 7]
    e_ref, stat_ref = refs[chunks + 7 : chunks + 9]
    scr_ref, r_ref, g_ref = refs[chunks + 9 :]
    n = i0_ref.shape[1]
    bins, pixels = tab_ref.shape
    lines = pixels // LINE_LEN
    half = 2 * chunks
    wide = 2 * half
    size = 4 * lines
    for s, p in enumerate(p_refs):
        scr_ref[s * size : (s + 1) * size] = p[...].astype(f32)
    cos_row, sin_row = trig_ref[0:1], trig_ref[1:2]
    power = [None] * half
    for l in range(lines):
        cols = slice(l * LINE_LEN, (l + 1) * LINE_LEN)
        x = jnp.concatenate(
            [scr_ref[pl.ds(2 * l + part, half, stride=2 * lines), :] for part in range(2)], axis=0
        )
        one = x * noise_ref[:, cols]
        r_ref[0:wide, cols] = one.astype(bf16)
        r_ref[wide : 2 * wide, cols] = (one * cos_row).astype(bf16)
        r_ref[2 * wide : 3 * wide, cols] = (one * sin_row).astype(bf16)
        square = one * x
        square = square[:half] + square[half:]
        t = tab_ref[:, cols].astype(f32)
        t = t * t
        for j in range(half):
            term = t * square[j : j + 1]
            power[j] = term if l == 0 else power[j] + term
    g_ref[:, : y_ref.shape[0]] = lax.dot_general(
        r_ref[...], y_ref[...], last_last, preferred_element_type=f32
    )
    step = 2 * n

    def left(v, k):
        return pltpu.roll(v, LINE_LEN - k, 1) if k else v

    def block(k):
        at = k * step // LINE_LEN * LINE_LEN
        return left(g_ref[: 3 * wide, at : at + LINE_LEN], k * step - at)

    even, odd = [], []
    for a in range(3):
        real, imag = block(2 * a), block(2 * a + 1)
        row = [(v * wide, v * wide + half, (v + 1) * wide) for v in range(3)]
        even.append([real[i:j] + imag[j:k] for i, j, k in row])
        odd.append([imag[i:j] - real[j:k] for i, j, k in row])
    onehot = onehot_of(i0_ref, i1_ref, bins)
    quad = 0.5 * jnp.concatenate(
        [
            jnp.sum(onehot * jnp.sum(p, axis=1, keepdims=True), axis=0, keepdims=True)
            for p in power
        ],
        axis=0,
    )
    pid = pid_ref[...]
    cand = spread(i0_ref[0:8], i1_ref[0:8])
    listed = cand[0:1] == pid
    for c in range(1, cand.shape[0]):
        listed = jnp.logical_or(listed, cand[c : c + 1] == pid)

    scores = []
    for a, sign in ((0, 0), (1, 1), (1, -1)):
        still, base, turn = even[a][0], even[a][1], odd[a][2]
        if sign == 1:
            still, base, turn = still + odd[2][0], base + odd[2][1], turn - even[2][2]
        if sign == -1:
            still, base, turn = still - odd[2][0], base - odd[2][1], turn + even[2][2]
        still, base = still - quad, base - quad
        scores.append([jnp.where(listed, v, -3.0e38) for v in (still, base + turn, base - turn)])
    peak = scores[0][0]
    for v in scores[0][1:] + scores[1] + scores[2]:
        peak = jnp.maximum(peak, v)
    peak = jnp.max(peak, axis=0, keepdims=True)
    terms = [[jnp.where(listed, jnp.exp(v - peak), 0.0) for v in group] for group in scores]
    total = 0.0
    for k, v in enumerate(terms[0] + terms[1] + terms[2]):
        total = total + v
        e_ref[k * half : (k + 1) * half] = v
    mass = jnp.sum(total, axis=0, keepdims=True)
    stat_ref[...] = jnp.concatenate([peak, mass, jnp.zeros((6, LINE_LEN), f32)], axis=0)


def coef_kernel(n, e_ref, m_ref, s_ref):
    half = e_ref.shape[0] // 9
    wide = 2 * half
    step = 2 * n

    def right(v, k):
        return pltpu.roll(v, k, 1) if k else v

    flat = [e_ref[k * half : (k + 1) * half] for k in range(9)]
    terms = [flat[0:3], flat[3:6], flat[6:9]]
    both = [p + m for _, p, m in terms]
    diff = [p - m for _, p, m in terms]
    still = [s for s, _, _ in terms]
    s_ref[...] = (still[0] + both[0]) + (still[1] + both[1]) + (still[2] + both[2])
    alpha = [
        [still[0], both[0], None],
        [still[1] + still[2], both[1] + both[2], None],
        [None, None, diff[2] - diff[1]],
    ]
    beta = [
        [None, None, diff[0]],
        [None, None, diff[1] + diff[2]],
        [still[1] - still[2], both[1] - both[2], None],
    ]
    zero = jnp.zeros((half, LINE_LEN), f32)
    for b in range(3):
        for at in range(0, 2 * LINE_LEN, LINE_LEN):
            real, imag = zero, zero
            for a in range(3):
                for part in range(2):
                    k = (2 * a + part) * step - at
                    if not 0 <= k < LINE_LEN:
                        continue
                    if alpha[a][b] is not None:
                        if part == 0:
                            real = real + right(alpha[a][b], k)
                        else:
                            imag = imag + right(alpha[a][b], k)
                    elif part == 0:
                        imag = imag - right(beta[a][b], k)
                    else:
                        real = real + right(beta[a][b], k)
            m_ref[b * wide : (b + 1) * wide, at : at + LINE_LEN] = by_chunk(real, imag)


def by_chunk(real, imag):
    pieces = []
    for s in range(real.shape[0] // 2):
        pieces += [real[2 * s : 2 * s + 2], imag[2 * s : 2 * s + 2]]
    return jnp.concatenate(pieces, axis=0)


def slice_kernel(
    y_ref, m_ref, s_ref, stat_ref, other_ref, i0_ref, i1_ref, trig_ref, keep_ref, *send_refs
):
    n = i0_ref.shape[1]
    pixels = y_ref.shape[1]
    half = s_ref.shape[0]
    wide = 2 * half
    lane = lax.broadcasted_iota(jnp.int32, (1, LINE_LEN), 1)
    other = other_ref[...]
    other = jnp.where(lane < n, pltpu.roll(other, LINE_LEN - n, 1), pltpu.roll(other, n, 1))
    peak0, mass0 = stat_ref[0:1], stat_ref[1:2]
    peak1, mass1 = other[0:1], other[1:2]
    peak = jnp.maximum(peak0, peak1)
    grow = jnp.exp(peak0 - peak)
    scale = grow / (mass0 * grow + mass1 * jnp.exp(peak1 - peak))
    scale = jnp.where(lane < 2 * n, scale, 0.0)
    share = lax.dot_general(
        s_ref[...] * scale,
        onehot_of(i0_ref, i1_ref, LINE_LEN),
        last_last,
        precision=exact,
        preferred_element_type=f32,
    )
    share = by_chunk(share, jnp.zeros_like(share))
    scales = scale
    for k in range(2 * n, LINE_LEN, 2 * n):
        scales = scales + pltpu.roll(scale, k, 1)
    m = m_ref[...] * jnp.concatenate([scales, scales], axis=1)
    m = m.astype(bf16)[:, : 12 * n]
    width = 1024
    cos_row = jnp.concatenate([trig_ref[0:1]] * (width // LINE_LEN), axis=1)
    sin_row = jnp.concatenate([trig_ref[1:2]] * (width // LINE_LEN), axis=1)
    for c in range(pixels // width):
        cols = slice(c * width, (c + 1) * width)
        x = jnp.dot(m, y_ref[:, cols], preferred_element_type=f32)
        x = x[:wide] + x[wide : 2 * wide] * cos_row + x[2 * wide :] * sin_row
        keep_ref[:, cols] = x[:4]
        for s, ref in enumerate(send_refs, 1):
            ref[:, cols] = x[4 * s : 4 * s + 4].astype(bf16)
    keep_ref[:, pixels:] = share[:4]
    for s, ref in enumerate(send_refs, 1):
        ref[:, pixels:] = share[4 * s : 4 * s + 4].astype(bf16)


def pack_kernel(lines, cap, chunks, slot_ref, own_ref, *refs):
    recv_refs = refs[: chunks - 1]
    keep_ref, *send_refs, scr_ref = refs[chunks - 1 :]
    size = 2 * cap
    for l in range(lines + 1):
        cols = slice(l * LINE_LEN, (l + 1) * LINE_LEN)
        x = own_ref[:, cols]
        for ref in recv_refs:
            x = x + ref[:, cols].astype(f32)
        if l < lines:
            for j in range(2):
                row = j * lines + l
                scr_ref[row : row + 1, :LINE_LEN] = x[j : j + 1]
                scr_ref[row : row + 1, LINE_LEN:] = x[2 + j : 3 + j]
        else:
            tail = jnp.concatenate([x, jnp.zeros((4, LINE_LEN), f32)], axis=0)
    slots = jnp.concatenate([slot_ref[0:1], slot_ref[1:2]], axis=1)
    rows = size * (len(send_refs) + 1)
    pick = slots == lax.broadcasted_iota(jnp.int32, (rows, 2 * lines), 0)
    packed = jnp.dot(
        pick.astype(f32).astype(bf16), scr_ref[...].astype(bf16), preferred_element_type=f32
    )
    for r, ref in enumerate([keep_ref] + send_refs):
        for part in range(2):
            piece = packed[r * size : (r + 1) * size, part * LINE_LEN : (part + 1) * LINE_LEN]
            ref[part * size : (part + 1) * size] = piece.astype(ref.dtype)
        ref[2 * size :] = tail.astype(ref.dtype)


def table_kernel(lines, cap, slot_ref, table_ref, sel_ref):
    bins = table_ref.shape[0]
    sel_ref[...] = jnp.zeros(sel_ref.shape, f32)
    for l in range(lines):
        t = table_ref[:, l * LINE_LEN : (l + 1) * LINE_LEN].astype(f32)
        t = t * t
        for j in range(2):
            slot = slot_ref[j, l]

            @pl.when(slot < 2 * cap)
            def _():
                sel_ref[j, pl.ds(slot - cap * j, bins, stride=cap), :] = t


def final_kernel(cap, bins, scale, own_ref, *refs):
    *recv_refs, sel_ref, data_hbm, weight_hbm, data_ref, weight_ref, sems = refs
    x = own_ref[...]
    for ref in recv_refs:
        x = x + ref[...].astype(f32)
    for part in range(2):
        for j in range(2):
            row = (2 * part + j) * cap
            data_ref[0, j, part] = x[row : row + cap]
    data_copy = pltpu.make_async_copy(data_ref, data_hbm, sems.at[0])
    data_copy.start()
    tail = x[4 * cap :] * scale
    for j in range(2):
        total = None
        for b in range(bins):
            term = sel_ref[j, b * cap : (b + 1) * cap] * tail[j : j + 1, b : b + 1]
            total = term if b == 0 else total + term
        weight_ref[0, j] = total
    weight_copy = pltpu.make_async_copy(weight_ref, weight_hbm, sems.at[1])
    weight_copy.start()
    data_copy.wait()
    weight_copy.wait()


def body(
    particles, defocus_bin, candidates, projections, ctf_table, inv_noise, line_slab, slab_owner
):
    n, _, pixels = particles.shape
    groups = lax.axis_size("grp")
    members = lax.axis_size("dev")
    chunks = members // 2
    lines = line_slab.shape[1]
    cap = 2 * lines // groups
    bins = ctf_table.shape[0]
    wide = 4 * chunks
    dev = lax.axis_index("dev")
    grp = lax.axis_index("grp")
    trig = jnp.asarray(trig_rows())
    noise = inv_noise[None, :]

    core = dev % 2
    chip_routes = routes(chunks, CHIP_ROUTES)
    group_routes = routes(groups, GROUP_ROUTES)

    def swap(x):
        return lax.ppermute(x, "dev", [(i, i ^ 1) for i in range(members)])

    def chip_pairs(t):
        return [(i, 2 * chip_routes[i % 2][t - 1][i // 2] + i % 2) for i in range(members)]

    def from_place(x, t):
        return lax.ppermute(x, "dev", [(j, i) for i, j in chip_pairs(t)])

    def to_place(x, t):
        return lax.ppermute(x, "dev", chip_pairs(t))

    def to_group(x, r):
        return lax.ppermute(
            x,
            ("grp", "dev"),
            [
                (g * members + i, group_routes[i % 2][r - 1][g] * members + i)
                for g in range(groups)
                for i in range(members)
            ],
        )

    def at_place(t, index, table):
        return jnp.where(core == 0, lookup(index, table[0][t - 1]), lookup(index, table[1][t - 1]))

    def as_lines(x):
        count = x.shape[0]
        x = x.reshape(count, 2, lines, LINE_LEN)
        return jnp.transpose(x, (0, 2, 1, 3)).reshape(2 * count * lines, LINE_LEN)

    part0, part1 = as_lines(particles), as_lines(swap(particles))
    proj = {t: from_place(projections, t) for t in range(1, chunks)}
    proj = [as_lines(p) for p in [projections] + [proj[t] for t in range(1, chunks)]]

    def in_hbm(x):
        return pltpu.with_memory_space_constraint(x, pltpu.HBM)

    vmem = pl.BlockSpec(memory_space=pltpu.VMEM)
    hbm = pl.BlockSpec(memory_space=pl.ANY)
    scratch = [pltpu.VMEM((2 * n * lines, LINE_LEN), f32), pltpu.VMEM((n, pixels), f32)]
    raw, table, ints0 = call(
        load_kernel,
        (
            jax.ShapeDtypeStruct(part0.shape, bf16),
            jax.ShapeDtypeStruct((bins, pixels), bf16),
            jax.ShapeDtypeStruct((16, n), jnp.int32),
        ),
        in_specs=[hbm] * 4,
        scratch_shapes=[
            pltpu.VMEM((8, n), jnp.int32),
            pltpu.VMEM((1, n), jnp.int32),
            pltpu.SemaphoreType.DMA((4,)),
        ],
        moved=32 * n * pixels,
    )(in_hbm(part0), in_hbm(ctf_table), in_hbm(candidates.T), in_hbm(defocus_bin[None, :]))
    ints1 = swap(ints0)
    y = call(
        own_kernel,
        jax.ShapeDtypeStruct((12 * n, pixels), bf16),
        scratch_shapes=scratch,
        flops=20 * n * pixels,
        moved=32 * n * pixels,
    )(raw, table, ints0)
    y = call(
        partner_kernel,
        jax.ShapeDtypeStruct((12 * n, pixels), bf16),
        in_specs=[vmem, vmem, vmem, hbm],
        scratch_shapes=scratch,
        input_output_aliases={3: 0},
        flops=20 * n * pixels,
        moved=32 * n * pixels,
    )(part1, table, ints1, y)

    row = lax.broadcasted_iota(jnp.int32, (2 * chunks, LINE_LEN), 0)
    chip = jnp.full(row.shape, dev // 2, jnp.int32)
    for t in range(1, chunks):
        chip = jnp.where(row // 2 == t, at_place(t, dev // 2, chip_routes), chip)
    pid = 4 * chip + 2 * core + row % 2
    terms, stat = call(
        functools.partial(score_kernel, chunks),
        (
            jax.ShapeDtypeStruct((18 * chunks, LINE_LEN), f32),
            jax.ShapeDtypeStruct((8, LINE_LEN), f32),
        ),
        scratch_shapes=[
            pltpu.VMEM((4 * lines * chunks, LINE_LEN), f32),
            pltpu.VMEM((3 * wide, pixels), bf16),
            pltpu.VMEM((3 * wide, 2 * LINE_LEN), f32),
        ],
        flops=2 * 192 * 3 * wide * pixels,
        moved=30 * n * pixels,
    )(*proj, y, table, ints0, ints1, noise, trig, pid)
    line_slab, stat = lax.optimization_barrier((line_slab, stat))
    other = swap(stat)
    m, share = call(
        functools.partial(coef_kernel, n),
        (
            jax.ShapeDtypeStruct((3 * wide, 2 * LINE_LEN), f32),
            jax.ShapeDtypeStruct((2 * chunks, LINE_LEN), f32),
        ),
        flops=100000,
        moved=100000,
    )(terms)
    own, *send = call(
        slice_kernel,
        (jax.ShapeDtypeStruct((4, pixels + LINE_LEN), f32),)
        + (jax.ShapeDtypeStruct((4, pixels + LINE_LEN), bf16),) * (chunks - 1),
        flops=2 * 192 * 3 * wide * pixels,
        moved=30 * n * pixels,
    )(y, m, share, stat, other, ints0, ints1, trig)
    got = [to_place(send[t - 1], t) for t in range(1, chunks)]

    group_ids = jnp.arange(groups, dtype=jnp.int32)
    slab_hit = line_slab[:, :, None] == group_ids[None, None, :]
    owner_line = jnp.sum(jnp.where(slab_hit, slab_owner[None, None, :], 0), axis=2)
    line_ids = jnp.arange(lines, dtype=jnp.int32)
    earlier = line_ids[None, :] < line_ids[:, None]
    same_owner = owner_line[:, :, None] == owner_line[:, None, :]
    line_rank = jnp.sum(jnp.logical_and(same_owner, earlier[None]), axis=2)
    place = jnp.zeros_like(owner_line)
    for r in range(1, groups):
        place = jnp.where(owner_line == at_place(r, grp, group_routes), r, place)
    slot = (2 * cap) * place + cap * jnp.arange(2, dtype=jnp.int32)[:, None] + line_rank
    slot = slot.astype(jnp.int32)

    sel = call(
        functools.partial(table_kernel, lines, cap),
        jax.ShapeDtypeStruct((2, bins * cap, LINE_LEN), f32),
        in_specs=[pl.BlockSpec(memory_space=pltpu.SMEM), vmem],
        flops=bins * pixels,
        moved=4 * bins * pixels,
    )(slot, table)
    size = 4 * cap + 8
    keep, *send = call(
        functools.partial(pack_kernel, lines, cap, chunks),
        (jax.ShapeDtypeStruct((size, LINE_LEN), f32),)
        + (jax.ShapeDtypeStruct((size, LINE_LEN), bf16),) * (groups - 1),
        scratch_shapes=[pltpu.VMEM((2 * lines, 2 * LINE_LEN), f32)],
        flops=16 * pixels,
        moved=64 * pixels,
    )(slot, own, *got)
    recv = [to_group(send[r - 1], r) for r in [groups - 1, *range(1, groups - 1)]]
    weight_scale = 2 * members / (n * groups * members)
    data, weight = (1, 2, 2, cap, LINE_LEN), (1, 2, cap, LINE_LEN)
    return call(
        functools.partial(final_kernel, cap, bins, weight_scale),
        (jax.ShapeDtypeStruct(data, f32), jax.ShapeDtypeStruct(weight, f32)),
        in_specs=[vmem] * (groups + 1),
        out_specs=(hbm, hbm),
        scratch_shapes=[
            pltpu.VMEM(data, f32),
            pltpu.VMEM(weight, f32),
            pltpu.SemaphoreType.DMA((2,)),
        ],
        flops=1000,
        moved=8 * 4 * cap * LINE_LEN,
    )(keep, *recv, sel)


def solution(mesh):
    return jax.shard_map(
        body,
        mesh=mesh,
        in_specs=(
            P(("grp", "dev"), None, None),
            P(("grp", "dev")),
            P(("grp", "dev"), None),
            P("dev", None, None),
            P(),
            P(),
            P("dev", None),
            P(),
        ),
        out_specs=(P("grp", "dev", None, None, None), P("grp", "dev", None, None)),
        check_vma=False,
    )
```

```python
import functools
import math

import jax
import jax.numpy as jnp
import numpy as np
from jax import lax
from jax.experimental import pallas as pl
from jax.experimental.pallas import tpu as pltpu
from jax.sharding import PartitionSpec as P

LINE_LEN = 128
STEP = 2.0 * math.pi / LINE_LEN
VMEM_BYTES = 40 * 1024 * 1024
f32 = jnp.float32
bf16 = jnp.bfloat16
exact = lax.Precision.HIGHEST
last_last = (((1,), (1,)), ((), ()))
first_first = (((0,), (0,)), ((), ()))


def trig_rows():
    column = np.arange(LINE_LEN)
    freq = np.where(column < LINE_LEN // 2, column, column - LINE_LEN)
    rows = np.zeros((8, LINE_LEN), np.float32)
    rows[0] = np.cos(freq * STEP)
    rows[1] = np.sin(freq * STEP)
    return rows


CHIP_ROUTES = [[[3, 2, 1, 0], [2, 3, 0, 1], [1, 0, 3, 2]], [[3, 2, 1, 0], [2, 3, 0, 1], [1, 0, 3, 2]]]
GROUP_ROUTES = [[[2, 3, 1, 0], [3, 2, 0, 1], [1, 0, 3, 2]], [[2, 3, 1, 0], [3, 2, 0, 1], [1, 0, 3, 2]]]


def routes(count, chosen):
    if count == 4:
        return chosen
    return [[[i ^ t for i in range(count)] for t in range(count - 1, 0, -1)]] * 2


def lookup(index, table):
    found = table[0]
    for i in range(1, len(table)):
        found = jnp.where(index == i, table[i], found)
    return found


def call(kernel, out_shape, flops=0, moved=0, **kw):
    return pl.pallas_call(
        kernel,
        out_shape=out_shape,
        compiler_params=pltpu.CompilerParams(vmem_limit_bytes=VMEM_BYTES),
        cost_estimate=pl.CostEstimate(flops=flops, bytes_accessed=moved, transcendentals=0),
        **kw,
    )


def spread(first, second):
    rows, n = first.shape
    rest = jnp.full((rows, LINE_LEN - 2 * n), -1, jnp.int32)
    return jnp.concatenate([first, second, rest], axis=1)


def onehot_of(i0_ref, i1_ref, bins):
    row = spread(i0_ref[8:9], i1_ref[8:9])
    return (row == lax.broadcasted_iota(jnp.int32, (bins, LINE_LEN), 0)).astype(f32)


def prep_half(place, step, part, defocus, tab_ref, y_ref, scr_ref, ctf_ref):
    n = defocus.shape[1]
    bins, pixels = tab_ref.shape
    lines = pixels // LINE_LEN
    onehot = (defocus == lax.broadcasted_iota(jnp.int32, (bins, n), 0)).astype(f32)
    scr_ref[...] = part.astype(f32)
    ctf_ref[...] = lax.dot_general(
        onehot.astype(bf16), tab_ref[...], first_first, preferred_element_type=f32
    )
    for l in range(lines):
        cols = slice(l * LINE_LEN, (l + 1) * LINE_LEN)
        ctf = ctf_ref[:, cols]
        for part in range(2):
            x = scr_ref[pl.ds(2 * l + part, n, stride=2 * lines), :] * ctf
            base = part * step + place
            y_ref[base : base + n, cols] = x.astype(bf16)
            base += 2 * step
            y_ref[base : base + n, cols] = (x * math.cos(l * STEP)).astype(bf16)
            base += 2 * step
            y_ref[base : base + n, cols] = (x * math.sin(l * STEP)).astype(bf16)


def mark_kernel(o_ref):
    o_ref[...] = jnp.zeros(o_ref.shape, jnp.int32)


def ints_kernel(c_ref, d_ref, mark_ref, ints_ref):
    ints_ref[0:8] = c_ref[...]
    ints_ref[8:] = jnp.broadcast_to(d_ref[...], (8, d_ref.shape[1])) + mark_ref[...]


def own_kernel(p_ref, tab_ref, d_ref, y_ref, scr_ref, ctf_ref):
    n = d_ref.shape[1]
    prep_half(0, n, p_ref[...], d_ref[8:9], tab_ref, y_ref, scr_ref, ctf_ref)


def partner_kernel(p_ref, tab_ref, d_ref, own_ref, y_ref, scr_ref, ctf_ref):
    n = d_ref.shape[1]
    prep_half(n, 2 * n, p_ref[...], d_ref[8:9], tab_ref, y_ref, scr_ref, ctf_ref)
    for k in range(6):
        y_ref[2 * k * n : (2 * k + 1) * n, :] = own_ref[k * n : (k + 1) * n, :]


def score_kernel(chunks, *refs):
    p_refs = refs[:chunks]
    y_ref, tab_ref, i0_ref, i1_ref, noise_ref, trig_ref, pid_ref = refs[chunks : chunks + 7]
    e_ref, stat_ref = refs[chunks + 7 : chunks + 9]
    scr_ref, r_ref, g_ref = refs[chunks + 9 :]
    n = i0_ref.shape[1]
    bins, pixels = tab_ref.shape
    lines = pixels // LINE_LEN
    half = 2 * chunks
    wide = 2 * half
    size = 4 * lines
    for s, p in enumerate(p_refs):
        scr_ref[s * size : (s + 1) * size] = p[...].astype(f32)
    cos_row, sin_row = trig_ref[0:1], trig_ref[1:2]
    power = [None] * half
    for l in range(lines):
        cols = slice(l * LINE_LEN, (l + 1) * LINE_LEN)
        x = jnp.concatenate(
            [scr_ref[pl.ds(2 * l + part, half, stride=2 * lines), :] for part in range(2)], axis=0
        )
        one = x * noise_ref[:, cols]
        r_ref[0:wide, cols] = one.astype(bf16)
        r_ref[wide : 2 * wide, cols] = (one * cos_row).astype(bf16)
        r_ref[2 * wide : 3 * wide, cols] = (one * sin_row).astype(bf16)
        square = one * x
        square = square[:half] + square[half:]
        t = tab_ref[:, cols].astype(f32)
        t = t * t
        for j in range(half):
            term = t * square[j : j + 1]
            power[j] = term if l == 0 else power[j] + term
    g_ref[:, : y_ref.shape[0]] = lax.dot_general(
        r_ref[...], y_ref[...], last_last, preferred_element_type=f32
    )
    step = 2 * n

    def left(v, k):
        return pltpu.roll(v, LINE_LEN - k, 1) if k else v

    def block(k):
        at = k * step // LINE_LEN * LINE_LEN
        return left(g_ref[: 3 * wide, at : at + LINE_LEN], k * step - at)

    even, odd = [], []
    for a in range(3):
        real, imag = block(2 * a), block(2 * a + 1)
        row = [(v * wide, v * wide + half, (v + 1) * wide) for v in range(3)]
        even.append([real[i:j] + imag[j:k] for i, j, k in row])
        odd.append([imag[i:j] - real[j:k] for i, j, k in row])
    onehot = onehot_of(i0_ref, i1_ref, bins)
    quad = 0.5 * jnp.concatenate(
        [
            jnp.sum(onehot * jnp.sum(p, axis=1, keepdims=True), axis=0, keepdims=True)
            for p in power
        ],
        axis=0,
    )
    pid = pid_ref[...]
    cand = spread(i0_ref[0:8], i1_ref[0:8])
    listed = cand[0:1] == pid
    for c in range(1, cand.shape[0]):
        listed = jnp.logical_or(listed, cand[c : c + 1] == pid)

    scores = []
    for a, sign in ((0, 0), (1, 1), (1, -1)):
        still, base, turn = even[a][0], even[a][1], odd[a][2]
        if sign == 1:
            still, base, turn = still + odd[2][0], base + odd[2][1], turn - even[2][2]
        if sign == -1:
            still, base, turn = still - odd[2][0], base - odd[2][1], turn + even[2][2]
        still, base = still - quad, base - quad
        scores.append([jnp.where(listed, v, -3.0e38) for v in (still, base + turn, base - turn)])
    peak = scores[0][0]
    for v in scores[0][1:] + scores[1] + scores[2]:
        peak = jnp.maximum(peak, v)
    peak = jnp.max(peak, axis=0, keepdims=True)
    terms = [[jnp.where(listed, jnp.exp(v - peak), 0.0) for v in group] for group in scores]
    total = 0.0
    for k, v in enumerate(terms[0] + terms[1] + terms[2]):
        total = total + v
        e_ref[k * half : (k + 1) * half] = v
    mass = jnp.sum(total, axis=0, keepdims=True)
    stat_ref[...] = jnp.concatenate([peak, mass, jnp.zeros((6, LINE_LEN), f32)], axis=0)


def coef_kernel(n, e_ref, m_ref, s_ref):
    half = e_ref.shape[0] // 9
    wide = 2 * half
    step = 2 * n

    def right(v, k):
        return pltpu.roll(v, k, 1) if k else v

    flat = [e_ref[k * half : (k + 1) * half] for k in range(9)]
    terms = [flat[0:3], flat[3:6], flat[6:9]]
    both = [p + m for _, p, m in terms]
    diff = [p - m for _, p, m in terms]
    still = [s for s, _, _ in terms]
    s_ref[...] = (still[0] + both[0]) + (still[1] + both[1]) + (still[2] + both[2])
    alpha = [
        [still[0], both[0], None],
        [still[1] + still[2], both[1] + both[2], None],
        [None, None, diff[2] - diff[1]],
    ]
    beta = [
        [None, None, diff[0]],
        [None, None, diff[1] + diff[2]],
        [still[1] - still[2], both[1] - both[2], None],
    ]
    zero = jnp.zeros((half, LINE_LEN), f32)
    for b in range(3):
        for at in range(0, 2 * LINE_LEN, LINE_LEN):
            real, imag = zero, zero
            for a in range(3):
                for part in range(2):
                    k = (2 * a + part) * step - at
                    if not 0 <= k < LINE_LEN:
                        continue
                    if alpha[a][b] is not None:
                        if part == 0:
                            real = real + right(alpha[a][b], k)
                        else:
                            imag = imag + right(alpha[a][b], k)
                    elif part == 0:
                        imag = imag - right(beta[a][b], k)
                    else:
                        real = real + right(beta[a][b], k)
            m_ref[b * wide : (b + 1) * wide, at : at + LINE_LEN] = by_chunk(real, imag)


def by_chunk(real, imag):
    pieces = []
    for s in range(real.shape[0] // 2):
        pieces += [real[2 * s : 2 * s + 2], imag[2 * s : 2 * s + 2]]
    return jnp.concatenate(pieces, axis=0)


def slice_kernel(
    y_ref, m_ref, s_ref, stat_ref, other_ref, i0_ref, i1_ref, trig_ref, keep_ref, *send_refs
):
    n = i0_ref.shape[1]
    pixels = y_ref.shape[1]
    half = s_ref.shape[0]
    wide = 2 * half
    lane = lax.broadcasted_iota(jnp.int32, (1, LINE_LEN), 1)
    other = other_ref[...]
    other = jnp.where(lane < n, pltpu.roll(other, LINE_LEN - n, 1), pltpu.roll(other, n, 1))
    peak0, mass0 = stat_ref[0:1], stat_ref[1:2]
    peak1, mass1 = other[0:1], other[1:2]
    peak = jnp.maximum(peak0, peak1)
    grow = jnp.exp(peak0 - peak)
    scale = grow / (mass0 * grow + mass1 * jnp.exp(peak1 - peak))
    scale = jnp.where(lane < 2 * n, scale, 0.0)
    share = lax.dot_general(
        s_ref[...] * scale,
        onehot_of(i0_ref, i1_ref, LINE_LEN),
        last_last,
        precision=exact,
        preferred_element_type=f32,
    )
    share = by_chunk(share, jnp.zeros_like(share))
    scales = scale
    for k in range(2 * n, LINE_LEN, 2 * n):
        scales = scales + pltpu.roll(scale, k, 1)
    m = m_ref[...] * jnp.concatenate([scales, scales], axis=1)
    m = m.astype(bf16)[:, : 12 * n]
    width = 1024
    cos_row = jnp.concatenate([trig_ref[0:1]] * (width // LINE_LEN), axis=1)
    sin_row = jnp.concatenate([trig_ref[1:2]] * (width // LINE_LEN), axis=1)
    for c in range(pixels // width):
        cols = slice(c * width, (c + 1) * width)
        x = jnp.dot(m, y_ref[:, cols], preferred_element_type=f32)
        x = x[:wide] + x[wide : 2 * wide] * cos_row + x[2 * wide :] * sin_row
        keep_ref[:, cols] = x[:4]
        for s, ref in enumerate(send_refs, 1):
            ref[:, cols] = x[4 * s : 4 * s + 4].astype(bf16)
    keep_ref[:, pixels:] = share[:4]
    for s, ref in enumerate(send_refs, 1):
        ref[:, pixels:] = share[4 * s : 4 * s + 4].astype(bf16)


def pack_kernel(lines, cap, chunks, slot_ref, own_ref, *refs):
    recv_refs = refs[: chunks - 1]
    keep_ref, *send_refs, scr_ref = refs[chunks - 1 :]
    size = 2 * cap
    for l in range(lines + 1):
        cols = slice(l * LINE_LEN, (l + 1) * LINE_LEN)
        x = own_ref[:, cols]
        for ref in recv_refs:
            x = x + ref[:, cols].astype(f32)
        if l < lines:
            for j in range(2):
                row = j * lines + l
                scr_ref[row : row + 1, :LINE_LEN] = x[j : j + 1]
                scr_ref[row : row + 1, LINE_LEN:] = x[2 + j : 3 + j]
        else:
            tail = jnp.concatenate([x, jnp.zeros((4, LINE_LEN), f32)], axis=0)
    slots = jnp.concatenate([slot_ref[0:1], slot_ref[1:2]], axis=1)
    rows = size * (len(send_refs) + 1)
    pick = slots == lax.broadcasted_iota(jnp.int32, (rows, 2 * lines), 0)
    packed = jnp.dot(
        pick.astype(f32).astype(bf16), scr_ref[...].astype(bf16), preferred_element_type=f32
    )
    for r, ref in enumerate([keep_ref] + send_refs):
        for part in range(2):
            piece = packed[r * size : (r + 1) * size, part * LINE_LEN : (part + 1) * LINE_LEN]
            ref[part * size : (part + 1) * size] = piece.astype(ref.dtype)
        ref[2 * size :] = tail.astype(ref.dtype)


def table_kernel(lines, cap, slot_ref, table_ref, sel_ref):
    bins = table_ref.shape[0]
    sel_ref[...] = jnp.zeros(sel_ref.shape, f32)
    for l in range(lines):
        t = table_ref[:, l * LINE_LEN : (l + 1) * LINE_LEN].astype(f32)
        t = t * t
        for j in range(2):
            slot = slot_ref[j, l]

            @pl.when(slot < 2 * cap)
            def _():
                sel_ref[j, pl.ds(slot - cap * j, bins, stride=cap), :] = t


def final_kernel(cap, bins, scale, own_ref, *refs):
    *recv_refs, sel_ref, data_ref, weight_ref = refs
    x = own_ref[...]
    for ref in recv_refs:
        x = x + ref[...].astype(f32)
    for part in range(2):
        for j in range(2):
            row = (2 * part + j) * cap
            data_ref[0, j, part] = x[row : row + cap]
    tail = x[4 * cap :] * scale
    for j in range(2):
        total = None
        for b in range(bins):
            term = sel_ref[j, b * cap : (b + 1) * cap] * tail[j : j + 1, b : b + 1]
            total = term if b == 0 else total + term
        weight_ref[0, j] = total


def body(
    particles, defocus_bin, candidates, projections, ctf_table, inv_noise, line_slab, slab_owner
):
    n, _, pixels = particles.shape
    groups = lax.axis_size("grp")
    members = lax.axis_size("dev")
    chunks = members // 2
    lines = line_slab.shape[1]
    cap = 2 * lines // groups
    bins = ctf_table.shape[0]
    wide = 4 * chunks
    dev = lax.axis_index("dev")
    grp = lax.axis_index("grp")
    trig = jnp.asarray(trig_rows())
    noise = inv_noise[None, :]

    core = dev % 2
    chip_routes = routes(chunks, CHIP_ROUTES)
    group_routes = routes(groups, GROUP_ROUTES)

    def swap(x):
        return lax.ppermute(x, "dev", [(i, i ^ 1) for i in range(members)])

    def chip_pairs(t):
        return [(i, 2 * chip_routes[i % 2][t - 1][i // 2] + i % 2) for i in range(members)]

    def from_place(x, t):
        return lax.ppermute(x, "dev", [(j, i) for i, j in chip_pairs(t)])

    def to_place(x, t):
        return lax.ppermute(x, "dev", chip_pairs(t))

    def to_group(x, r):
        return lax.ppermute(
            x,
            ("grp", "dev"),
            [
                (g * members + i, group_routes[i % 2][r - 1][g] * members + i)
                for g in range(groups)
                for i in range(members)
            ],
        )

    def at_place(t, index, table):
        return jnp.where(core == 0, lookup(index, table[0][t - 1]), lookup(index, table[1][t - 1]))

    def as_lines(x):
        count = x.shape[0]
        x = x.reshape(count, 2, lines, LINE_LEN)
        return jnp.transpose(x, (0, 2, 1, 3)).reshape(2 * count * lines, LINE_LEN)

    part0, part1 = as_lines(particles), as_lines(swap(particles))
    proj = {t: from_place(projections, t) for t in range(1, chunks)}
    proj = [as_lines(p) for p in [projections] + [proj[t] for t in range(1, chunks)]]

    vmem = pl.BlockSpec(memory_space=pltpu.VMEM)
    scratch = [pltpu.VMEM((2 * n * lines, LINE_LEN), f32), pltpu.VMEM((n, pixels), f32)]
    mark = call(
        mark_kernel, jax.ShapeDtypeStruct((8, n), jnp.int32), flops=20000000000, moved=1000
    )()
    ints0 = call(
        ints_kernel,
        jax.ShapeDtypeStruct((16, n), jnp.int32),
        in_specs=[vmem] * 3,
        moved=1000,
    )(candidates.T, defocus_bin[None, :], mark)
    ints1 = swap(ints0)
    own_rows = call(
        own_kernel,
        jax.ShapeDtypeStruct((6 * n, pixels), bf16),
        scratch_shapes=scratch,
        flops=20 * n * pixels,
        moved=32 * n * pixels,
    )(part0, ctf_table, ints0)
    y = call(
        partner_kernel,
        jax.ShapeDtypeStruct((12 * n, pixels), bf16),
        scratch_shapes=scratch,
        flops=20 * n * pixels,
        moved=32 * n * pixels,
    )(part1, ctf_table, ints1, own_rows)

    row = lax.broadcasted_iota(jnp.int32, (2 * chunks, LINE_LEN), 0)
    chip = jnp.full(row.shape, dev // 2, jnp.int32)
    for t in range(1, chunks):
        chip = jnp.where(row // 2 == t, at_place(t, dev // 2, chip_routes), chip)
    pid = 4 * chip + 2 * core + row % 2
    terms, stat = call(
        functools.partial(score_kernel, chunks),
        (
            jax.ShapeDtypeStruct((18 * chunks, LINE_LEN), f32),
            jax.ShapeDtypeStruct((8, LINE_LEN), f32),
        ),
        scratch_shapes=[
            pltpu.VMEM((4 * lines * chunks, LINE_LEN), f32),
            pltpu.VMEM((3 * wide, pixels), bf16),
            pltpu.VMEM((3 * wide, 2 * LINE_LEN), f32),
        ],
        flops=2 * 192 * 3 * wide * pixels,
        moved=30 * n * pixels,
    )(*proj, y, ctf_table, ints0, ints1, noise, trig, pid)
    line_slab, stat = lax.optimization_barrier((line_slab, stat))
    other = swap(stat)
    m, share = call(
        functools.partial(coef_kernel, n),
        (
            jax.ShapeDtypeStruct((3 * wide, 2 * LINE_LEN), f32),
            jax.ShapeDtypeStruct((2 * chunks, LINE_LEN), f32),
        ),
        flops=100000,
        moved=100000,
    )(terms)
    own, *send = call(
        slice_kernel,
        (jax.ShapeDtypeStruct((4, pixels + LINE_LEN), f32),)
        + (jax.ShapeDtypeStruct((4, pixels + LINE_LEN), bf16),) * (chunks - 1),
        flops=2 * 192 * 3 * wide * pixels,
        moved=30 * n * pixels,
    )(y, m, share, stat, other, ints0, ints1, trig)
    got = [to_place(send[t - 1], t) for t in range(1, chunks)]

    group_ids = jnp.arange(groups, dtype=jnp.int32)
    slab_hit = line_slab[:, :, None] == group_ids[None, None, :]
    owner_line = jnp.sum(jnp.where(slab_hit, slab_owner[None, None, :], 0), axis=2)
    line_ids = jnp.arange(lines, dtype=jnp.int32)
    earlier = line_ids[None, :] < line_ids[:, None]
    same_owner = owner_line[:, :, None] == owner_line[:, None, :]
    line_rank = jnp.sum(jnp.logical_and(same_owner, earlier[None]), axis=2)
    place = jnp.zeros_like(owner_line)
    for r in range(1, groups):
        place = jnp.where(owner_line == at_place(r, grp, group_routes), r, place)
    slot = (2 * cap) * place + cap * jnp.arange(2, dtype=jnp.int32)[:, None] + line_rank
    slot = slot.astype(jnp.int32)

    sel = call(
        functools.partial(table_kernel, lines, cap),
        jax.ShapeDtypeStruct((2, bins * cap, LINE_LEN), f32),
        in_specs=[pl.BlockSpec(memory_space=pltpu.SMEM), vmem],
        flops=bins * pixels,
        moved=4 * bins * pixels,
    )(slot, ctf_table)
    size = 4 * cap + 8
    keep, *send = call(
        functools.partial(pack_kernel, lines, cap, chunks),
        (jax.ShapeDtypeStruct((size, LINE_LEN), f32),)
        + (jax.ShapeDtypeStruct((size, LINE_LEN), bf16),) * (groups - 1),
        scratch_shapes=[pltpu.VMEM((2 * lines, 2 * LINE_LEN), f32)],
        flops=16 * pixels,
        moved=64 * pixels,
    )(slot, own, *got)
    recv = [to_group(send[r - 1], r) for r in [groups - 1, *range(1, groups - 1)]]
    weight_scale = 2 * members / (n * groups * members)
    data, weight = (1, 2, 2, cap, LINE_LEN), (1, 2, cap, LINE_LEN)
    return call(
        functools.partial(final_kernel, cap, bins, weight_scale),
        (jax.ShapeDtypeStruct(data, f32), jax.ShapeDtypeStruct(weight, f32)),
        in_specs=[vmem] * (groups + 1),
        flops=1000,
        moved=8 * 4 * cap * LINE_LEN,
    )(keep, *recv, sel)


def solution(mesh):
    return jax.shard_map(
        body,
        mesh=mesh,
        in_specs=(
            P(("grp", "dev"), None, None),
            P(("grp", "dev")),
            P(("grp", "dev"), None),
            P("dev", None, None),
            P(),
            P(),
            P("dev", None),
            P(),
        ),
        out_specs=(P("grp", "dev", None, None, None), P("grp", "dev", None, None)),
        check_vma=False,
    )
```

```python
import functools
import math

import jax
import jax.numpy as jnp
import numpy as np
from jax import lax
from jax.experimental import pallas as pl
from jax.experimental.pallas import tpu as pltpu
from jax.sharding import PartitionSpec as P

LINE_LEN = 128
STEP = 2.0 * math.pi / LINE_LEN
VMEM_BYTES = 40 * 1024 * 1024
f32 = jnp.float32
bf16 = jnp.bfloat16
exact = lax.Precision.HIGHEST
last_last = (((1,), (1,)), ((), ()))
first_first = (((0,), (0,)), ((), ()))


def trig_rows():
    column = np.arange(LINE_LEN)
    freq = np.where(column < LINE_LEN // 2, column, column - LINE_LEN)
    rows = np.zeros((8, LINE_LEN), np.float32)
    rows[0] = np.cos(freq * STEP)
    rows[1] = np.sin(freq * STEP)
    return rows


CHIP_ROUTES = [[[2, 3, 0, 1], [1, 0, 3, 2], [3, 2, 1, 0]], [[2, 3, 0, 1], [1, 0, 3, 2], [3, 2, 1, 0]]]
GROUP_ROUTES = [[[2, 3, 1, 0], [3, 2, 0, 1], [1, 0, 3, 2]], [[2, 3, 1, 0], [3, 2, 0, 1], [1, 0, 3, 2]]]


def routes(count, chosen):
    if count == 4:
        return chosen
    return [[[i ^ t for i in range(count)] for t in range(count - 1, 0, -1)]] * 2


def lookup(index, table):
    found = table[0]
    for i in range(1, len(table)):
        found = jnp.where(index == i, table[i], found)
    return found


def call(kernel, out_shape, flops=0, moved=0, **kw):
    return pl.pallas_call(
        kernel,
        out_shape=out_shape,
        compiler_params=pltpu.CompilerParams(vmem_limit_bytes=VMEM_BYTES),
        cost_estimate=pl.CostEstimate(flops=flops, bytes_accessed=moved, transcendentals=0),
        **kw,
    )


def spread(first, second):
    rows, n = first.shape
    rest = jnp.full((rows, LINE_LEN - 2 * n), -1, jnp.int32)
    return jnp.concatenate([first, second, rest], axis=1)


def onehot_of(i0_ref, i1_ref, bins):
    row = spread(i0_ref[8:9], i1_ref[8:9])
    return (row == lax.broadcasted_iota(jnp.int32, (bins, LINE_LEN), 0)).astype(f32)


def prep_half(place, step, part, defocus, tab_ref, y_ref, scr_ref, ctf_ref):
    n = defocus.shape[1]
    bins, pixels = tab_ref.shape
    lines = pixels // LINE_LEN
    onehot = (defocus == lax.broadcasted_iota(jnp.int32, (bins, n), 0)).astype(f32)
    scr_ref[...] = part.astype(f32)
    ctf_ref[...] = lax.dot_general(
        onehot.astype(bf16), tab_ref[...], first_first, preferred_element_type=f32
    )
    for l in range(lines):
        cols = slice(l * LINE_LEN, (l + 1) * LINE_LEN)
        ctf = ctf_ref[:, cols]
        for part in range(2):
            x = scr_ref[pl.ds(2 * l + part, n, stride=2 * lines), :] * ctf
            base = part * step + place
            y_ref[base : base + n, cols] = x.astype(bf16)
            base += 2 * step
            y_ref[base : base + n, cols] = (x * math.cos(l * STEP)).astype(bf16)
            base += 2 * step
            y_ref[base : base + n, cols] = (x * math.sin(l * STEP)).astype(bf16)


def mark_kernel(o_ref):
    o_ref[...] = jnp.zeros(o_ref.shape, jnp.int32)


def ints_kernel(c_ref, d_ref, mark_ref, ints_ref):
    ints_ref[0:8] = c_ref[...]
    ints_ref[8:] = jnp.broadcast_to(d_ref[...], (8, d_ref.shape[1])) + mark_ref[...]


def own_kernel(p_ref, tab_ref, d_ref, y_ref, scr_ref, ctf_ref):
    n = d_ref.shape[1]
    prep_half(0, n, p_ref[...], d_ref[8:9], tab_ref, y_ref, scr_ref, ctf_ref)


def partner_kernel(p_ref, tab_ref, d_ref, own_ref, y_ref, scr_ref, ctf_ref):
    n = d_ref.shape[1]
    prep_half(n, 2 * n, p_ref[...], d_ref[8:9], tab_ref, y_ref, scr_ref, ctf_ref)
    for k in range(6):
        y_ref[2 * k * n : (2 * k + 1) * n, :] = own_ref[k * n : (k + 1) * n, :]


def score_kernel(chunks, *refs):
    p_refs = refs[:chunks]
    y_ref, tab_ref, i0_ref, i1_ref, noise_ref, trig_ref, pid_ref = refs[chunks : chunks + 7]
    e_ref, stat_ref = refs[chunks + 7 : chunks + 9]
    scr_ref, r_ref, g_ref = refs[chunks + 9 :]
    n = i0_ref.shape[1]
    bins, pixels = tab_ref.shape
    lines = pixels // LINE_LEN
    half = 2 * chunks
    wide = 2 * half
    size = 4 * lines
    for s, p in enumerate(p_refs):
        scr_ref[s * size : (s + 1) * size] = p[...].astype(f32)
    cos_row, sin_row = trig_ref[0:1], trig_ref[1:2]
    power = [None] * half
    for l in range(lines):
        cols = slice(l * LINE_LEN, (l + 1) * LINE_LEN)
        x = jnp.concatenate(
            [scr_ref[pl.ds(2 * l + part, half, stride=2 * lines), :] for part in range(2)], axis=0
        )
        one = x * noise_ref[:, cols]
        r_ref[0:wide, cols] = one.astype(bf16)
        r_ref[wide : 2 * wide, cols] = (one * cos_row).astype(bf16)
        r_ref[2 * wide : 3 * wide, cols] = (one * sin_row).astype(bf16)
        square = one * x
        square = square[:half] + square[half:]
        t = tab_ref[:, cols].astype(f32)
        t = t * t
        for j in range(half):
            term = t * square[j : j + 1]
            power[j] = term if l == 0 else power[j] + term
    g_ref[:, : y_ref.shape[0]] = lax.dot_general(
        r_ref[...], y_ref[...], last_last, preferred_element_type=f32
    )
    step = 2 * n

    def left(v, k):
        return pltpu.roll(v, LINE_LEN - k, 1) if k else v

    def block(k):
        at = k * step // LINE_LEN * LINE_LEN
        return left(g_ref[: 3 * wide, at : at + LINE_LEN], k * step - at)

    even, odd = [], []
    for a in range(3):
        real, imag = block(2 * a), block(2 * a + 1)
        row = [(v * wide, v * wide + half, (v + 1) * wide) for v in range(3)]
        even.append([real[i:j] + imag[j:k] for i, j, k in row])
        odd.append([imag[i:j] - real[j:k] for i, j, k in row])
    onehot = onehot_of(i0_ref, i1_ref, bins)
    quad = 0.5 * jnp.concatenate(
        [
            jnp.sum(onehot * jnp.sum(p, axis=1, keepdims=True), axis=0, keepdims=True)
            for p in power
        ],
        axis=0,
    )
    pid = pid_ref[...]
    cand = spread(i0_ref[0:8], i1_ref[0:8])
    listed = cand[0:1] == pid
    for c in range(1, cand.shape[0]):
        listed = jnp.logical_or(listed, cand[c : c + 1] == pid)

    scores = []
    for a, sign in ((0, 0), (1, 1), (1, -1)):
        still, base, turn = even[a][0], even[a][1], odd[a][2]
        if sign == 1:
            still, base, turn = still + odd[2][0], base + odd[2][1], turn - even[2][2]
        if sign == -1:
            still, base, turn = still - odd[2][0], base - odd[2][1], turn + even[2][2]
        still, base = still - quad, base - quad
        scores.append([jnp.where(listed, v, -3.0e38) for v in (still, base + turn, base - turn)])
    peak = scores[0][0]
    for v in scores[0][1:] + scores[1] + scores[2]:
        peak = jnp.maximum(peak, v)
    peak = jnp.max(peak, axis=0, keepdims=True)
    terms = [[jnp.where(listed, jnp.exp(v - peak), 0.0) for v in group] for group in scores]
    total = 0.0
    for k, v in enumerate(terms[0] + terms[1] + terms[2]):
        total = total + v
        e_ref[k * half : (k + 1) * half] = v
    mass = jnp.sum(total, axis=0, keepdims=True)
    stat_ref[...] = jnp.concatenate([peak, mass, jnp.zeros((6, LINE_LEN), f32)], axis=0)


def coef_kernel(n, e_ref, m_ref, s_ref):
    half = e_ref.shape[0] // 9
    wide = 2 * half
    step = 2 * n

    def right(v, k):
        return pltpu.roll(v, k, 1) if k else v

    flat = [e_ref[k * half : (k + 1) * half] for k in range(9)]
    terms = [flat[0:3], flat[3:6], flat[6:9]]
    both = [p + m for _, p, m in terms]
    diff = [p - m for _, p, m in terms]
    still = [s for s, _, _ in terms]
    s_ref[...] = (still[0] + both[0]) + (still[1] + both[1]) + (still[2] + both[2])
    alpha = [
        [still[0], both[0], None],
        [still[1] + still[2], both[1] + both[2], None],
        [None, None, diff[2] - diff[1]],
    ]
    beta = [
        [None, None, diff[0]],
        [None, None, diff[1] + diff[2]],
        [still[1] - still[2], both[1] - both[2], None],
    ]
    zero = jnp.zeros((half, LINE_LEN), f32)
    for b in range(3):
        for at in range(0, 2 * LINE_LEN, LINE_LEN):
            real, imag = zero, zero
            for a in range(3):
                for part in range(2):
                    k = (2 * a + part) * step - at
                    if not 0 <= k < LINE_LEN:
                        continue
                    if alpha[a][b] is not None:
                        if part == 0:
                            real = real + right(alpha[a][b], k)
                        else:
                            imag = imag + right(alpha[a][b], k)
                    elif part == 0:
                        imag = imag - right(beta[a][b], k)
                    else:
                        real = real + right(beta[a][b], k)
            m_ref[b * wide : (b + 1) * wide, at : at + LINE_LEN] = by_chunk(real, imag)


def by_chunk(real, imag):
    pieces = []
    for s in range(real.shape[0] // 2):
        pieces += [real[2 * s : 2 * s + 2], imag[2 * s : 2 * s + 2]]
    return jnp.concatenate(pieces, axis=0)


def slice_kernel(
    y_ref, m_ref, s_ref, stat_ref, other_ref, i0_ref, i1_ref, trig_ref, *send_refs
):
    n = i0_ref.shape[1]
    pixels = y_ref.shape[1]
    half = s_ref.shape[0]
    wide = 2 * half
    lane = lax.broadcasted_iota(jnp.int32, (1, LINE_LEN), 1)
    other = other_ref[...]
    other = jnp.where(lane < n, pltpu.roll(other, LINE_LEN - n, 1), pltpu.roll(other, n, 1))
    peak0, mass0 = stat_ref[0:1], stat_ref[1:2]
    peak1, mass1 = other[0:1], other[1:2]
    peak = jnp.maximum(peak0, peak1)
    grow = jnp.exp(peak0 - peak)
    scale = grow / (mass0 * grow + mass1 * jnp.exp(peak1 - peak))
    scale = jnp.where(lane < 2 * n, scale, 0.0)
    share = lax.dot_general(
        s_ref[...] * scale,
        onehot_of(i0_ref, i1_ref, LINE_LEN),
        last_last,
        precision=exact,
        preferred_element_type=f32,
    )
    share = by_chunk(share, jnp.zeros_like(share))
    scales = scale
    for k in range(2 * n, LINE_LEN, 2 * n):
        scales = scales + pltpu.roll(scale, k, 1)
    m = m_ref[...] * jnp.concatenate([scales, scales], axis=1)
    m = m.astype(bf16)[:, : 12 * n]
    width = 1024
    cos_row = jnp.concatenate([trig_ref[0:1]] * (width // LINE_LEN), axis=1)
    sin_row = jnp.concatenate([trig_ref[1:2]] * (width // LINE_LEN), axis=1)
    for c in range(pixels // width):
        cols = slice(c * width, (c + 1) * width)
        x = jnp.dot(m, y_ref[:, cols], preferred_element_type=f32)
        x = x[:wide] + x[wide : 2 * wide] * cos_row + x[2 * wide :] * sin_row
        for s, ref in enumerate(send_refs):
            ref[:, cols] = x[4 * s : 4 * s + 4].astype(bf16)
    for s, ref in enumerate(send_refs):
        ref[:, pixels:] = share[4 * s : 4 * s + 4].astype(bf16)


def pack_kernel(lines, cap, chunks, slot_ref, own_ref, *refs):
    recv_refs = refs[: chunks - 1]
    *send_refs, scr_ref = refs[chunks - 1 :]
    size = 2 * cap
    for l in range(lines + 1):
        cols = slice(l * LINE_LEN, (l + 1) * LINE_LEN)
        x = own_ref[:, cols].astype(f32)
        for ref in recv_refs:
            x = x + ref[:, cols].astype(f32)
        if l < lines:
            for j in range(2):
                row = j * lines + l
                scr_ref[row : row + 1, :LINE_LEN] = x[j : j + 1]
                scr_ref[row : row + 1, LINE_LEN:] = x[2 + j : 3 + j]
        else:
            tail = jnp.concatenate([x, jnp.zeros((4, LINE_LEN), f32)], axis=0)
    slots = jnp.concatenate([slot_ref[0:1], slot_ref[1:2]], axis=1)
    rows = size * len(send_refs)
    pick = slots == lax.broadcasted_iota(jnp.int32, (rows, 2 * lines), 0)
    packed = jnp.dot(
        pick.astype(f32).astype(bf16), scr_ref[...].astype(bf16), preferred_element_type=f32
    )
    for r, ref in enumerate(send_refs):
        for part in range(2):
            piece = packed[r * size : (r + 1) * size, part * LINE_LEN : (part + 1) * LINE_LEN]
            ref[part * size : (part + 1) * size] = piece.astype(ref.dtype)
        ref[2 * size :] = tail.astype(ref.dtype)


def table_kernel(lines, cap, slot_ref, table_ref, sel_ref):
    bins = table_ref.shape[0]
    sel_ref[...] = jnp.zeros(sel_ref.shape, f32)
    for l in range(lines):
        t = table_ref[:, l * LINE_LEN : (l + 1) * LINE_LEN].astype(f32)
        t = t * t
        for j in range(2):
            slot = slot_ref[j, l]

            @pl.when(slot < 2 * cap)
            def _():
                sel_ref[j, pl.ds(slot - cap * j, bins, stride=cap), :] = t


def final_kernel(cap, bins, scale, own_ref, *refs):
    *recv_refs, sel_ref, data_ref, weight_ref = refs
    x = own_ref[...].astype(f32)
    for ref in recv_refs:
        x = x + ref[...].astype(f32)
    for part in range(2):
        for j in range(2):
            row = (2 * part + j) * cap
            data_ref[0, j, part] = x[row : row + cap]
    tail = x[4 * cap :] * scale
    for j in range(2):
        total = None
        for b in range(bins):
            term = sel_ref[j, b * cap : (b + 1) * cap] * tail[j : j + 1, b : b + 1]
            total = term if b == 0 else total + term
        weight_ref[0, j] = total


def body(
    particles, defocus_bin, candidates, projections, ctf_table, inv_noise, line_slab, slab_owner
):
    n, _, pixels = particles.shape
    groups = lax.axis_size("grp")
    members = lax.axis_size("dev")
    chunks = members // 2
    lines = line_slab.shape[1]
    cap = 2 * lines // groups
    bins = ctf_table.shape[0]
    wide = 4 * chunks
    dev = lax.axis_index("dev")
    grp = lax.axis_index("grp")
    trig = jnp.asarray(trig_rows())
    noise = inv_noise[None, :]

    core = dev % 2
    chip_routes = routes(chunks, CHIP_ROUTES)
    group_routes = routes(groups, GROUP_ROUTES)

    def swap(x):
        return lax.ppermute(x, "dev", [(i, i ^ 1) for i in range(members)])

    def chip_pairs(t):
        return [(i, 2 * chip_routes[i % 2][t - 1][i // 2] + i % 2) for i in range(members)]

    def from_place(x, t):
        return lax.ppermute(x, "dev", [(j, i) for i, j in chip_pairs(t)])

    def to_place(x, t):
        return lax.ppermute(x, "dev", [(i, j ^ 1) for i, j in chip_pairs(t)])

    def to_group(x, r):
        return lax.ppermute(
            x,
            ("grp", "dev"),
            [
                (g * members + i, group_routes[i % 2][r - 1][g] * members + (i ^ 1))
                for g in range(groups)
                for i in range(members)
            ],
        )

    def at_place(t, index, table):
        return jnp.where(core == 0, lookup(index, table[0][t - 1]), lookup(index, table[1][t - 1]))

    def as_lines(x):
        count = x.shape[0]
        x = x.reshape(count, 2, lines, LINE_LEN)
        return jnp.transpose(x, (0, 2, 1, 3)).reshape(2 * count * lines, LINE_LEN)

    part0, part1 = as_lines(particles), as_lines(swap(particles))
    proj = {t: from_place(projections, t) for t in range(1, chunks)}
    proj = [as_lines(p) for p in [projections] + [proj[t] for t in range(1, chunks)]]

    vmem = pl.BlockSpec(memory_space=pltpu.VMEM)
    scratch = [pltpu.VMEM((2 * n * lines, LINE_LEN), f32), pltpu.VMEM((n, pixels), f32)]
    mark = call(
        mark_kernel, jax.ShapeDtypeStruct((8, n), jnp.int32), flops=20000000000, moved=1000
    )()
    ints0 = call(
        ints_kernel,
        jax.ShapeDtypeStruct((16, n), jnp.int32),
        in_specs=[vmem] * 3,
        moved=1000,
    )(candidates.T, defocus_bin[None, :], mark)
    ints1 = swap(ints0)
    own_rows = call(
        own_kernel,
        jax.ShapeDtypeStruct((6 * n, pixels), bf16),
        scratch_shapes=scratch,
        flops=20 * n * pixels,
        moved=32 * n * pixels,
    )(part0, ctf_table, ints0)
    y = call(
        partner_kernel,
        jax.ShapeDtypeStruct((12 * n, pixels), bf16),
        scratch_shapes=scratch,
        flops=20 * n * pixels,
        moved=32 * n * pixels,
    )(part1, ctf_table, ints1, own_rows)

    row = lax.broadcasted_iota(jnp.int32, (2 * chunks, LINE_LEN), 0)
    chip = jnp.full(row.shape, dev // 2, jnp.int32)
    for t in range(1, chunks):
        chip = jnp.where(row // 2 == t, at_place(t, dev // 2, chip_routes), chip)
    pid = 4 * chip + 2 * core + row % 2
    terms, stat = call(
        functools.partial(score_kernel, chunks),
        (
            jax.ShapeDtypeStruct((18 * chunks, LINE_LEN), f32),
            jax.ShapeDtypeStruct((8, LINE_LEN), f32),
        ),
        scratch_shapes=[
            pltpu.VMEM((4 * lines * chunks, LINE_LEN), f32),
            pltpu.VMEM((3 * wide, pixels), bf16),
            pltpu.VMEM((3 * wide, 2 * LINE_LEN), f32),
        ],
        flops=2 * 192 * 3 * wide * pixels,
        moved=30 * n * pixels,
    )(*proj, y, ctf_table, ints0, ints1, noise, trig, pid)
    line_slab, stat = lax.optimization_barrier((line_slab, stat))
    other = swap(stat)
    m, share = call(
        functools.partial(coef_kernel, n),
        (
            jax.ShapeDtypeStruct((3 * wide, 2 * LINE_LEN), f32),
            jax.ShapeDtypeStruct((2 * chunks, LINE_LEN), f32),
        ),
        flops=100000,
        moved=100000,
    )(terms)
    send = call(
        slice_kernel,
        (jax.ShapeDtypeStruct((4, pixels + LINE_LEN), bf16),) * chunks,
        flops=2 * 192 * 3 * wide * pixels,
        moved=30 * n * pixels,
    )(y, m, share, stat, other, ints0, ints1, trig)
    got = [to_place(send[t], t) for t in range(1, chunks)]
    own = swap(send[0])

    group_ids = jnp.arange(groups, dtype=jnp.int32)
    slab_hit = line_slab[:, :, None] == group_ids[None, None, :]
    owner_line = jnp.sum(jnp.where(slab_hit, slab_owner[None, None, :], 0), axis=2)
    line_ids = jnp.arange(lines, dtype=jnp.int32)
    earlier = line_ids[None, :] < line_ids[:, None]
    same_owner = owner_line[:, :, None] == owner_line[:, None, :]
    line_rank = jnp.sum(jnp.logical_and(same_owner, earlier[None]), axis=2)
    place = jnp.zeros_like(owner_line)
    for r in range(1, groups):
        place = jnp.where(owner_line == at_place(r, grp, group_routes), r, place)
    slot = (2 * cap) * place + cap * jnp.arange(2, dtype=jnp.int32)[:, None] + line_rank
    slot = slot.astype(jnp.int32)

    sel = call(
        functools.partial(table_kernel, lines, cap),
        jax.ShapeDtypeStruct((2, bins * cap, LINE_LEN), f32),
        in_specs=[pl.BlockSpec(memory_space=pltpu.SMEM), vmem],
        flops=bins * pixels,
        moved=4 * bins * pixels,
    )(slot, ctf_table)
    size = 4 * cap + 8
    send = call(
        functools.partial(pack_kernel, lines, cap, chunks),
        (jax.ShapeDtypeStruct((size, LINE_LEN), bf16),) * groups,
        scratch_shapes=[pltpu.VMEM((2 * lines, 2 * LINE_LEN), f32)],
        flops=16 * pixels,
        moved=64 * pixels,
    )(swap(slot), own, *got)
    recv = [to_group(send[r], r) for r in range(1, groups)]
    keep = swap(send[0])
    weight_scale = 2 * members / (n * groups * members)
    data, weight = (1, 2, 2, cap, LINE_LEN), (1, 2, cap, LINE_LEN)
    return call(
        functools.partial(final_kernel, cap, bins, weight_scale),
        (jax.ShapeDtypeStruct(data, f32), jax.ShapeDtypeStruct(weight, f32)),
        in_specs=[vmem] * (groups + 1),
        flops=1000,
        moved=8 * 4 * cap * LINE_LEN,
    )(keep, *recv, sel)


def solution(mesh):
    return jax.shard_map(
        body,
        mesh=mesh,
        in_specs=(
            P(("grp", "dev"), None, None),
            P(("grp", "dev")),
            P(("grp", "dev"), None),
            P("dev", None, None),
            P(),
            P(),
            P("dev", None),
            P(),
        ),
        out_specs=(P("grp", "dev", None, None, None), P("grp", "dev", None, None)),
        check_vma=False,
    )
```

```python
import functools
import math

import jax
import jax.numpy as jnp
import numpy as np
from jax import lax
from jax.experimental import pallas as pl
from jax.experimental.pallas import tpu as pltpu
from jax.sharding import PartitionSpec as P

LINE_LEN = 128
STEP = 2.0 * math.pi / LINE_LEN
VMEM_BYTES = 40 * 1024 * 1024
f32 = jnp.float32
bf16 = jnp.bfloat16
exact = lax.Precision.HIGHEST
last_last = (((1,), (1,)), ((), ()))
first_first = (((0,), (0,)), ((), ()))


def trig_rows():
    column = np.arange(LINE_LEN)
    freq = np.where(column < LINE_LEN // 2, column, column - LINE_LEN)
    rows = np.zeros((8, LINE_LEN), np.float32)
    rows[0] = np.cos(freq * STEP)
    rows[1] = np.sin(freq * STEP)
    return rows


CHIP_ROUTES = [[[2, 3, 0, 1], [1, 0, 3, 2], [3, 2, 1, 0]], [[2, 3, 0, 1], [1, 0, 3, 2], [3, 2, 1, 0]]]
GROUP_ROUTES = [[[1, 2, 3, 0], [2, 3, 0, 1], [3, 0, 1, 2]], [[1, 2, 3, 0], [2, 3, 0, 1], [3, 0, 1, 2]]]


def routes(count, chosen):
    if count == 4:
        return chosen
    return [[[i ^ t for i in range(count)] for t in range(count - 1, 0, -1)]] * 2


def lookup(index, table):
    found = table[0]
    for i in range(1, len(table)):
        found = jnp.where(index == i, table[i], found)
    return found


def call(kernel, out_shape, flops=0, moved=0, **kw):
    return pl.pallas_call(
        kernel,
        out_shape=out_shape,
        compiler_params=pltpu.CompilerParams(vmem_limit_bytes=VMEM_BYTES),
        cost_estimate=pl.CostEstimate(flops=flops, bytes_accessed=moved, transcendentals=0),
        **kw,
    )


def spread(first, second):
    rows, n = first.shape
    rest = jnp.full((rows, LINE_LEN - 2 * n), -1, jnp.int32)
    return jnp.concatenate([first, second, rest], axis=1)


def onehot_of(i0_ref, i1_ref, bins):
    row = spread(i0_ref[8:9], i1_ref[8:9])
    return (row == lax.broadcasted_iota(jnp.int32, (bins, LINE_LEN), 0)).astype(f32)


def prep_half(place, step, part, defocus, tab_ref, y_ref, scr_ref, ctf_ref):
    n = defocus.shape[1]
    bins, pixels = tab_ref.shape
    lines = pixels // LINE_LEN
    onehot = (defocus == lax.broadcasted_iota(jnp.int32, (bins, n), 0)).astype(f32)
    scr_ref[...] = part.astype(f32)
    ctf_ref[...] = lax.dot_general(
        onehot.astype(bf16), tab_ref[...], first_first, preferred_element_type=f32
    )
    for l in range(lines):
        cols = slice(l * LINE_LEN, (l + 1) * LINE_LEN)
        ctf = ctf_ref[:, cols]
        for part in range(2):
            x = scr_ref[pl.ds(2 * l + part, n, stride=2 * lines), :] * ctf
            base = part * step + place
            y_ref[base : base + n, cols] = x.astype(bf16)
            base += 2 * step
            y_ref[base : base + n, cols] = (x * math.cos(l * STEP)).astype(bf16)
            base += 2 * step
            y_ref[base : base + n, cols] = (x * math.sin(l * STEP)).astype(bf16)


def mark_kernel(o_ref):
    o_ref[...] = jnp.zeros(o_ref.shape, jnp.int32)


def ints_kernel(c_ref, d_ref, mark_ref, ints_ref):
    ints_ref[0:8] = c_ref[...]
    ints_ref[8:] = jnp.broadcast_to(d_ref[...], (8, d_ref.shape[1])) + mark_ref[...]


def own_kernel(p_ref, tab_ref, d_ref, y_ref, scr_ref, ctf_ref):
    n = d_ref.shape[1]
    prep_half(0, n, p_ref[...], d_ref[8:9], tab_ref, y_ref, scr_ref, ctf_ref)


def partner_kernel(p_ref, tab_ref, d_ref, own_ref, y_ref, scr_ref, ctf_ref):
    n = d_ref.shape[1]
    prep_half(n, 2 * n, p_ref[...], d_ref[8:9], tab_ref, y_ref, scr_ref, ctf_ref)
    for k in range(6):
        y_ref[2 * k * n : (2 * k + 1) * n, :] = own_ref[k * n : (k + 1) * n, :]


def score_kernel(chunks, *refs):
    p_refs = refs[:chunks]
    y_ref, tab_ref, i0_ref, i1_ref, noise_ref, trig_ref, pid_ref = refs[chunks : chunks + 7]
    e_ref, stat_ref = refs[chunks + 7 : chunks + 9]
    scr_ref, r_ref, g_ref = refs[chunks + 9 :]
    n = i0_ref.shape[1]
    bins, pixels = tab_ref.shape
    lines = pixels // LINE_LEN
    half = 2 * chunks
    wide = 2 * half
    size = 4 * lines
    for s, p in enumerate(p_refs):
        scr_ref[s * size : (s + 1) * size] = p[...].astype(f32)
    cos_row, sin_row = trig_ref[0:1], trig_ref[1:2]
    power = [None] * half
    for l in range(lines):
        cols = slice(l * LINE_LEN, (l + 1) * LINE_LEN)
        x = jnp.concatenate(
            [scr_ref[pl.ds(2 * l + part, half, stride=2 * lines), :] for part in range(2)], axis=0
        )
        one = x * noise_ref[:, cols]
        r_ref[0:wide, cols] = one.astype(bf16)
        r_ref[wide : 2 * wide, cols] = (one * cos_row).astype(bf16)
        r_ref[2 * wide : 3 * wide, cols] = (one * sin_row).astype(bf16)
        square = one * x
        square = square[:half] + square[half:]
        t = tab_ref[:, cols].astype(f32)
        t = t * t
        for j in range(half):
            term = t * square[j : j + 1]
            power[j] = term if l == 0 else power[j] + term
    g_ref[:, : y_ref.shape[0]] = lax.dot_general(
        r_ref[...], y_ref[...], last_last, preferred_element_type=f32
    )
    step = 2 * n

    def left(v, k):
        return pltpu.roll(v, LINE_LEN - k, 1) if k else v

    def block(k):
        at = k * step // LINE_LEN * LINE_LEN
        return left(g_ref[: 3 * wide, at : at + LINE_LEN], k * step - at)

    even, odd = [], []
    for a in range(3):
        real, imag = block(2 * a), block(2 * a + 1)
        row = [(v * wide, v * wide + half, (v + 1) * wide) for v in range(3)]
        even.append([real[i:j] + imag[j:k] for i, j, k in row])
        odd.append([imag[i:j] - real[j:k] for i, j, k in row])
    onehot = onehot_of(i0_ref, i1_ref, bins)
    quad = 0.5 * jnp.concatenate(
        [
            jnp.sum(onehot * jnp.sum(p, axis=1, keepdims=True), axis=0, keepdims=True)
            for p in power
        ],
        axis=0,
    )
    pid = pid_ref[...]
    cand = spread(i0_ref[0:8], i1_ref[0:8])
    listed = cand[0:1] == pid
    for c in range(1, cand.shape[0]):
        listed = jnp.logical_or(listed, cand[c : c + 1] == pid)

    scores = []
    for a, sign in ((0, 0), (1, 1), (1, -1)):
        still, base, turn = even[a][0], even[a][1], odd[a][2]
        if sign == 1:
            still, base, turn = still + odd[2][0], base + odd[2][1], turn - even[2][2]
        if sign == -1:
            still, base, turn = still - odd[2][0], base - odd[2][1], turn + even[2][2]
        still, base = still - quad, base - quad
        scores.append([jnp.where(listed, v, -3.0e38) for v in (still, base + turn, base - turn)])
    peak = scores[0][0]
    for v in scores[0][1:] + scores[1] + scores[2]:
        peak = jnp.maximum(peak, v)
    peak = jnp.max(peak, axis=0, keepdims=True)
    terms = [[jnp.where(listed, jnp.exp(v - peak), 0.0) for v in group] for group in scores]
    total = 0.0
    for k, v in enumerate(terms[0] + terms[1] + terms[2]):
        total = total + v
        e_ref[k * half : (k + 1) * half] = v
    mass = jnp.sum(total, axis=0, keepdims=True)
    stat_ref[...] = jnp.concatenate([peak, mass, jnp.zeros((6, LINE_LEN), f32)], axis=0)


def coef_kernel(n, e_ref, m_ref, s_ref):
    half = e_ref.shape[0] // 9
    wide = 2 * half
    step = 2 * n

    def right(v, k):
        return pltpu.roll(v, k, 1) if k else v

    flat = [e_ref[k * half : (k + 1) * half] for k in range(9)]
    terms = [flat[0:3], flat[3:6], flat[6:9]]
    both = [p + m for _, p, m in terms]
    diff = [p - m for _, p, m in terms]
    still = [s for s, _, _ in terms]
    s_ref[...] = (still[0] + both[0]) + (still[1] + both[1]) + (still[2] + both[2])
    alpha = [
        [still[0], both[0], None],
        [still[1] + still[2], both[1] + both[2], None],
        [None, None, diff[2] - diff[1]],
    ]
    beta = [
        [None, None, diff[0]],
        [None, None, diff[1] + diff[2]],
        [still[1] - still[2], both[1] - both[2], None],
    ]
    zero = jnp.zeros((half, LINE_LEN), f32)
    for b in range(3):
        for at in range(0, 2 * LINE_LEN, LINE_LEN):
            real, imag = zero, zero
            for a in range(3):
                for part in range(2):
                    k = (2 * a + part) * step - at
                    if not 0 <= k < LINE_LEN:
                        continue
                    if alpha[a][b] is not None:
                        if part == 0:
                            real = real + right(alpha[a][b], k)
                        else:
                            imag = imag + right(alpha[a][b], k)
                    elif part == 0:
                        imag = imag - right(beta[a][b], k)
                    else:
                        real = real + right(beta[a][b], k)
            m_ref[b * wide : (b + 1) * wide, at : at + LINE_LEN] = by_chunk(real, imag)


def by_chunk(real, imag):
    pieces = []
    for s in range(real.shape[0] // 2):
        pieces += [real[2 * s : 2 * s + 2], imag[2 * s : 2 * s + 2]]
    return jnp.concatenate(pieces, axis=0)


def slice_kernel(
    y_ref, m_ref, s_ref, stat_ref, other_ref, i0_ref, i1_ref, trig_ref, *send_refs
):
    n = i0_ref.shape[1]
    pixels = y_ref.shape[1]
    half = s_ref.shape[0]
    wide = 2 * half
    lane = lax.broadcasted_iota(jnp.int32, (1, LINE_LEN), 1)
    other = other_ref[...]
    other = jnp.where(lane < n, pltpu.roll(other, LINE_LEN - n, 1), pltpu.roll(other, n, 1))
    peak0, mass0 = stat_ref[0:1], stat_ref[1:2]
    peak1, mass1 = other[0:1], other[1:2]
    peak = jnp.maximum(peak0, peak1)
    grow = jnp.exp(peak0 - peak)
    scale = grow / (mass0 * grow + mass1 * jnp.exp(peak1 - peak))
    scale = jnp.where(lane < 2 * n, scale, 0.0)
    share = lax.dot_general(
        s_ref[...] * scale,
        onehot_of(i0_ref, i1_ref, LINE_LEN),
        last_last,
        precision=exact,
        preferred_element_type=f32,
    )
    share = by_chunk(share, jnp.zeros_like(share))
    scales = scale
    for k in range(2 * n, LINE_LEN, 2 * n):
        scales = scales + pltpu.roll(scale, k, 1)
    m = m_ref[...] * jnp.concatenate([scales, scales], axis=1)
    m = m.astype(bf16)[:, : 12 * n]
    width = 1024
    cos_row = jnp.concatenate([trig_ref[0:1]] * (width // LINE_LEN), axis=1)
    sin_row = jnp.concatenate([trig_ref[1:2]] * (width // LINE_LEN), axis=1)
    for c in range(pixels // width):
        cols = slice(c * width, (c + 1) * width)
        x = jnp.dot(m, y_ref[:, cols], preferred_element_type=f32)
        x = x[:wide] + x[wide : 2 * wide] * cos_row + x[2 * wide :] * sin_row
        for s, ref in enumerate(send_refs):
            ref[:, cols] = x[4 * s : 4 * s + 4].astype(bf16)
    for s, ref in enumerate(send_refs):
        ref[:, pixels:] = share[4 * s : 4 * s + 4].astype(bf16)


def pack_kernel(lines, cap, chunks, slot_ref, own_ref, *refs):
    recv_refs = refs[: chunks - 1]
    *send_refs, scr_ref = refs[chunks - 1 :]
    size = 2 * cap
    for l in range(lines + 1):
        cols = slice(l * LINE_LEN, (l + 1) * LINE_LEN)
        x = own_ref[:, cols].astype(f32)
        for ref in recv_refs:
            x = x + ref[:, cols].astype(f32)
        if l < lines:
            for j in range(2):
                row = j * lines + l
                scr_ref[row : row + 1, :LINE_LEN] = x[j : j + 1]
                scr_ref[row : row + 1, LINE_LEN:] = x[2 + j : 3 + j]
        else:
            tail = jnp.concatenate([x, jnp.zeros((4, LINE_LEN), f32)], axis=0)
    slots = jnp.concatenate([slot_ref[0:1], slot_ref[1:2]], axis=1)
    rows = size * len(send_refs)
    pick = slots == lax.broadcasted_iota(jnp.int32, (rows, 2 * lines), 0)
    packed = jnp.dot(
        pick.astype(f32).astype(bf16), scr_ref[...].astype(bf16), preferred_element_type=f32
    )
    for r, ref in enumerate(send_refs):
        for part in range(2):
            piece = packed[r * size : (r + 1) * size, part * LINE_LEN : (part + 1) * LINE_LEN]
            ref[part * size : (part + 1) * size] = piece.astype(ref.dtype)
        ref[2 * size :] = tail.astype(ref.dtype)


def table_kernel(lines, cap, slot_ref, table_ref, sel_ref):
    bins = table_ref.shape[0]
    sel_ref[...] = jnp.zeros(sel_ref.shape, f32)
    for l in range(lines):
        t = table_ref[:, l * LINE_LEN : (l + 1) * LINE_LEN].astype(f32)
        t = t * t
        for j in range(2):
            slot = slot_ref[j, l]

            @pl.when(slot < 2 * cap)
            def _():
                sel_ref[j, pl.ds(slot - cap * j, bins, stride=cap), :] = t


def final_kernel(cap, bins, scale, own_ref, *refs):
    *recv_refs, sel_ref, data_ref, weight_ref = refs
    x = own_ref[...].astype(f32)
    for ref in recv_refs:
        x = x + ref[...].astype(f32)
    for part in range(2):
        for j in range(2):
            row = (2 * part + j) * cap
            data_ref[0, j, part] = x[row : row + cap]
    tail = x[4 * cap :] * scale
    for j in range(2):
        total = None
        for b in range(bins):
            term = sel_ref[j, b * cap : (b + 1) * cap] * tail[j : j + 1, b : b + 1]
            total = term if b == 0 else total + term
        weight_ref[0, j] = total


def body(
    particles, defocus_bin, candidates, projections, ctf_table, inv_noise, line_slab, slab_owner
):
    n, _, pixels = particles.shape
    groups = lax.axis_size("grp")
    members = lax.axis_size("dev")
    chunks = members // 2
    lines = line_slab.shape[1]
    cap = 2 * lines // groups
    bins = ctf_table.shape[0]
    wide = 4 * chunks
    dev = lax.axis_index("dev")
    grp = lax.axis_index("grp")
    trig = jnp.asarray(trig_rows())
    noise = inv_noise[None, :]

    core = dev % 2
    chip_routes = routes(chunks, CHIP_ROUTES)
    group_routes = routes(groups, GROUP_ROUTES)

    def swap(x):
        return lax.ppermute(x, "dev", [(i, i ^ 1) for i in range(members)])

    def chip_pairs(t):
        return [(i, 2 * chip_routes[i % 2][t - 1][i // 2] + i % 2) for i in range(members)]

    def from_place(x, t):
        return lax.ppermute(x, "dev", [(j, i) for i, j in chip_pairs(t)])

    def to_place(x, t):
        return lax.ppermute(x, "dev", [(i, j ^ 1) for i, j in chip_pairs(t)])

    def to_group(x, r):
        return lax.ppermute(
            x,
            ("grp", "dev"),
            [
                (g * members + i, group_routes[i % 2][r - 1][g] * members + (i ^ 1))
                for g in range(groups)
                for i in range(members)
            ],
        )

    def at_place(t, index, table):
        return jnp.where(core == 0, lookup(index, table[0][t - 1]), lookup(index, table[1][t - 1]))

    def as_lines(x):
        count = x.shape[0]
        x = x.reshape(count, 2, lines, LINE_LEN)
        return jnp.transpose(x, (0, 2, 1, 3)).reshape(2 * count * lines, LINE_LEN)

    part0, part1 = as_lines(particles), as_lines(swap(particles))
    proj = {t: from_place(projections, t) for t in range(1, chunks)}
    proj = [as_lines(p) for p in [projections] + [proj[t] for t in range(1, chunks)]]

    vmem = pl.BlockSpec(memory_space=pltpu.VMEM)
    scratch = [pltpu.VMEM((2 * n * lines, LINE_LEN), f32), pltpu.VMEM((n, pixels), f32)]
    mark = call(
        mark_kernel, jax.ShapeDtypeStruct((8, n), jnp.int32), flops=20000000000, moved=1000
    )()
    ints0 = call(
        ints_kernel,
        jax.ShapeDtypeStruct((16, n), jnp.int32),
        in_specs=[vmem] * 3,
        moved=1000,
    )(candidates.T, defocus_bin[None, :], mark)
    ints1 = swap(ints0)
    own_rows = call(
        own_kernel,
        jax.ShapeDtypeStruct((6 * n, pixels), bf16),
        scratch_shapes=scratch,
        flops=20 * n * pixels,
        moved=32 * n * pixels,
    )(part0, ctf_table, ints0)
    y = call(
        partner_kernel,
        jax.ShapeDtypeStruct((12 * n, pixels), bf16),
        scratch_shapes=scratch,
        flops=20 * n * pixels,
        moved=32 * n * pixels,
    )(part1, ctf_table, ints1, own_rows)

    row = lax.broadcasted_iota(jnp.int32, (2 * chunks, LINE_LEN), 0)
    chip = jnp.full(row.shape, dev // 2, jnp.int32)
    for t in range(1, chunks):
        chip = jnp.where(row // 2 == t, at_place(t, dev // 2, chip_routes), chip)
    pid = 4 * chip + 2 * core + row % 2
    terms, stat = call(
        functools.partial(score_kernel, chunks),
        (
            jax.ShapeDtypeStruct((18 * chunks, LINE_LEN), f32),
            jax.ShapeDtypeStruct((8, LINE_LEN), f32),
        ),
        scratch_shapes=[
            pltpu.VMEM((4 * lines * chunks, LINE_LEN), f32),
            pltpu.VMEM((3 * wide, pixels), bf16),
            pltpu.VMEM((3 * wide, 2 * LINE_LEN), f32),
        ],
        flops=2 * 192 * 3 * wide * pixels,
        moved=30 * n * pixels,
    )(*proj, y, ctf_table, ints0, ints1, noise, trig, pid)
    line_slab, stat = lax.optimization_barrier((line_slab, stat))
    other = swap(stat)
    m, share = call(
        functools.partial(coef_kernel, n),
        (
            jax.ShapeDtypeStruct((3 * wide, 2 * LINE_LEN), f32),
            jax.ShapeDtypeStruct((2 * chunks, LINE_LEN), f32),
        ),
        flops=100000,
        moved=100000,
    )(terms)
    send = call(
        slice_kernel,
        (jax.ShapeDtypeStruct((4, pixels + LINE_LEN), bf16),) * chunks,
        flops=2 * 192 * 3 * wide * pixels,
        moved=30 * n * pixels,
    )(y, m, share, stat, other, ints0, ints1, trig)
    got = [to_place(send[t], t) for t in range(1, chunks)]
    own = swap(send[0])

    group_ids = jnp.arange(groups, dtype=jnp.int32)
    slab_hit = line_slab[:, :, None] == group_ids[None, None, :]
    owner_line = jnp.sum(jnp.where(slab_hit, slab_owner[None, None, :], 0), axis=2)
    line_ids = jnp.arange(lines, dtype=jnp.int32)
    earlier = line_ids[None, :] < line_ids[:, None]
    same_owner = owner_line[:, :, None] == owner_line[:, None, :]
    line_rank = jnp.sum(jnp.logical_and(same_owner, earlier[None]), axis=2)
    place = jnp.zeros_like(owner_line)
    for r in range(1, groups):
        place = jnp.where(owner_line == at_place(r, grp, group_routes), r, place)
    slot = (2 * cap) * place + cap * jnp.arange(2, dtype=jnp.int32)[:, None] + line_rank
    slot = slot.astype(jnp.int32)

    sel = call(
        functools.partial(table_kernel, lines, cap),
        jax.ShapeDtypeStruct((2, bins * cap, LINE_LEN), f32),
        in_specs=[pl.BlockSpec(memory_space=pltpu.SMEM), vmem],
        flops=bins * pixels,
        moved=4 * bins * pixels,
    )(slot, ctf_table)
    size = 4 * cap + 8
    send = call(
        functools.partial(pack_kernel, lines, cap, chunks),
        (jax.ShapeDtypeStruct((size, LINE_LEN), bf16),) * groups,
        scratch_shapes=[pltpu.VMEM((2 * lines, 2 * LINE_LEN), f32)],
        flops=16 * pixels,
        moved=64 * pixels,
    )(swap(slot), own, *got)
    recv = [to_group(send[r], r) for r in range(1, groups)]
    keep = swap(send[0])
    weight_scale = 2 * members / (n * groups * members)
    data, weight = (1, 2, 2, cap, LINE_LEN), (1, 2, cap, LINE_LEN)
    return call(
        functools.partial(final_kernel, cap, bins, weight_scale),
        (jax.ShapeDtypeStruct(data, f32), jax.ShapeDtypeStruct(weight, f32)),
        in_specs=[vmem] * (groups + 1),
        flops=1000,
        moved=8 * 4 * cap * LINE_LEN,
    )(keep, *recv, sel)


def solution(mesh):
    return jax.shard_map(
        body,
        mesh=mesh,
        in_specs=(
            P(("grp", "dev"), None, None),
            P(("grp", "dev")),
            P(("grp", "dev"), None),
            P("dev", None, None),
            P(),
            P(),
            P("dev", None),
            P(),
        ),
        out_specs=(P("grp", "dev", None, None, None), P("grp", "dev", None, None)),
        check_vma=False,
    )
```

```python
import functools
import math

import jax
import jax.numpy as jnp
import numpy as np
from jax import lax
from jax.experimental import pallas as pl
from jax.experimental.pallas import tpu as pltpu
from jax.sharding import PartitionSpec as P

LINE_LEN = 128
STEP = 2.0 * math.pi / LINE_LEN
VMEM_BYTES = 40 * 1024 * 1024
f32 = jnp.float32
bf16 = jnp.bfloat16
exact = lax.Precision.HIGHEST
last_last = (((1,), (1,)), ((), ()))
first_first = (((0,), (0,)), ((), ()))


def trig_rows():
    column = np.arange(LINE_LEN)
    freq = np.where(column < LINE_LEN // 2, column, column - LINE_LEN)
    rows = np.zeros((8, LINE_LEN), np.float32)
    rows[0] = np.cos(freq * STEP)
    rows[1] = np.sin(freq * STEP)
    return rows


CHIP_ROUTES = [[[2, 3, 0, 1], [1, 0, 3, 2], [3, 2, 1, 0]], [[2, 3, 0, 1], [1, 0, 3, 2], [3, 2, 1, 0]]]
GROUP_ROUTES = [[[1, 2, 3, 0], [2, 3, 0, 1], [3, 0, 1, 2]], [[1, 2, 3, 0], [2, 3, 0, 1], [3, 0, 1, 2]]]


def routes(count, chosen):
    if count == 4:
        return chosen
    return [[[i ^ t for i in range(count)] for t in range(count - 1, 0, -1)]] * 2


def lookup(index, table):
    found = table[0]
    for i in range(1, len(table)):
        found = jnp.where(index == i, table[i], found)
    return found


def call(kernel, out_shape, flops=0, moved=0, **kw):
    return pl.pallas_call(
        kernel,
        out_shape=out_shape,
        compiler_params=pltpu.CompilerParams(vmem_limit_bytes=VMEM_BYTES),
        cost_estimate=pl.CostEstimate(flops=flops, bytes_accessed=moved, transcendentals=0),
        **kw,
    )


def spread(first, second):
    rows, n = first.shape
    rest = jnp.full((rows, LINE_LEN - 2 * n), -1, jnp.int32)
    return jnp.concatenate([first, second, rest], axis=1)


def onehot_of(i0_ref, i1_ref, bins):
    row = spread(i0_ref[8:9], i1_ref[8:9])
    return (row == lax.broadcasted_iota(jnp.int32, (bins, LINE_LEN), 0)).astype(f32)


def prep_half(place, step, part, defocus, tab_ref, y_ref, scr_ref, ctf_ref):
    n = defocus.shape[1]
    bins, pixels = tab_ref.shape
    lines = pixels // LINE_LEN
    onehot = (defocus == lax.broadcasted_iota(jnp.int32, (bins, n), 0)).astype(f32)
    scr_ref[...] = part.astype(f32)
    ctf_ref[...] = lax.dot_general(
        onehot.astype(bf16), tab_ref[...], first_first, preferred_element_type=f32
    )
    for l in range(lines):
        cols = slice(l * LINE_LEN, (l + 1) * LINE_LEN)
        ctf = ctf_ref[:, cols]
        for part in range(2):
            x = scr_ref[pl.ds(2 * l + part, n, stride=2 * lines), :] * ctf
            base = part * step + place
            y_ref[base : base + n, cols] = x.astype(bf16)
            base += 2 * step
            y_ref[base : base + n, cols] = (x * math.cos(l * STEP)).astype(bf16)
            base += 2 * step
            y_ref[base : base + n, cols] = (x * math.sin(l * STEP)).astype(bf16)


def mark_kernel(o_ref):
    o_ref[...] = jnp.zeros(o_ref.shape, jnp.int32)


def ints_kernel(c_ref, d_ref, mark_ref, ints_ref):
    ints_ref[0:8] = c_ref[...]
    ints_ref[8:] = jnp.broadcast_to(d_ref[...], (8, d_ref.shape[1])) + mark_ref[...]


def own_kernel(p_ref, tab_ref, d_ref, y_ref, scr_ref, ctf_ref):
    n = d_ref.shape[1]
    prep_half(0, n, p_ref[...], d_ref[8:9], tab_ref, y_ref, scr_ref, ctf_ref)


def partner_kernel(p_ref, tab_ref, d_ref, own_ref, y_ref, scr_ref, ctf_ref):
    n = d_ref.shape[1]
    prep_half(n, 2 * n, p_ref[...], d_ref[8:9], tab_ref, y_ref, scr_ref, ctf_ref)
    for k in range(6):
        y_ref[2 * k * n : (2 * k + 1) * n, :] = own_ref[k * n : (k + 1) * n, :]


def score_kernel(chunks, *refs):
    p_refs = refs[:chunks]
    y_ref, tab_ref, i0_ref, i1_ref, noise_ref, trig_ref, pid_ref = refs[chunks : chunks + 7]
    e_ref, stat_ref = refs[chunks + 7 : chunks + 9]
    scr_ref, r_ref, g_ref = refs[chunks + 9 :]
    n = i0_ref.shape[1]
    bins, pixels = tab_ref.shape
    lines = pixels // LINE_LEN
    half = 2 * chunks
    wide = 2 * half
    size = 4 * lines
    for s, p in enumerate(p_refs):
        scr_ref[s * size : (s + 1) * size] = p[...].astype(f32)
    cos_row, sin_row = trig_ref[0:1], trig_ref[1:2]
    power = [None] * half
    for l in range(lines):
        cols = slice(l * LINE_LEN, (l + 1) * LINE_LEN)
        x = jnp.concatenate(
            [scr_ref[pl.ds(2 * l + part, half, stride=2 * lines), :] for part in range(2)], axis=0
        )
        one = x * noise_ref[:, cols]
        r_ref[0:wide, cols] = one.astype(bf16)
        r_ref[wide : 2 * wide, cols] = (one * cos_row).astype(bf16)
        r_ref[2 * wide : 3 * wide, cols] = (one * sin_row).astype(bf16)
        square = one * x
        square = square[:half] + square[half:]
        t = tab_ref[:, cols].astype(f32)
        t = t * t
        for j in range(half):
            term = t * square[j : j + 1]
            power[j] = term if l == 0 else power[j] + term
    g_ref[:, : y_ref.shape[0]] = lax.dot_general(
        r_ref[...], y_ref[...], last_last, preferred_element_type=f32
    )
    step = 2 * n

    def left(v, k):
        return pltpu.roll(v, LINE_LEN - k, 1) if k else v

    def block(k):
        at = k * step // LINE_LEN * LINE_LEN
        return left(g_ref[: 3 * wide, at : at + LINE_LEN], k * step - at)

    even, odd = [], []
    for a in range(3):
        real, imag = block(2 * a), block(2 * a + 1)
        row = [(v * wide, v * wide + half, (v + 1) * wide) for v in range(3)]
        even.append([real[i:j] + imag[j:k] for i, j, k in row])
        odd.append([imag[i:j] - real[j:k] for i, j, k in row])
    onehot = onehot_of(i0_ref, i1_ref, bins)
    quad = 0.5 * jnp.concatenate(
        [
            jnp.sum(onehot * jnp.sum(p, axis=1, keepdims=True), axis=0, keepdims=True)
            for p in power
        ],
        axis=0,
    )
    pid = pid_ref[...]
    cand = spread(i0_ref[0:8], i1_ref[0:8])
    listed = cand[0:1] == pid
    for c in range(1, cand.shape[0]):
        listed = jnp.logical_or(listed, cand[c : c + 1] == pid)

    scores = []
    for a, sign in ((0, 0), (1, 1), (1, -1)):
        still, base, turn = even[a][0], even[a][1], odd[a][2]
        if sign == 1:
            still, base, turn = still + odd[2][0], base + odd[2][1], turn - even[2][2]
        if sign == -1:
            still, base, turn = still - odd[2][0], base - odd[2][1], turn + even[2][2]
        still, base = still - quad, base - quad
        scores.append([jnp.where(listed, v, -3.0e38) for v in (still, base + turn, base - turn)])
    peak = scores[0][0]
    for v in scores[0][1:] + scores[1] + scores[2]:
        peak = jnp.maximum(peak, v)
    peak = jnp.max(peak, axis=0, keepdims=True)
    terms = [[jnp.where(listed, jnp.exp(v - peak), 0.0) for v in group] for group in scores]
    total = 0.0
    for k, v in enumerate(terms[0] + terms[1] + terms[2]):
        total = total + v
        e_ref[k * half : (k + 1) * half] = v
    mass = jnp.sum(total, axis=0, keepdims=True)
    stat_ref[...] = jnp.concatenate([peak, mass, jnp.zeros((6, LINE_LEN), f32)], axis=0)


def coef_kernel(n, e_ref, m_ref, s_ref):
    half = e_ref.shape[0] // 9
    wide = 2 * half
    step = 2 * n

    def right(v, k):
        return pltpu.roll(v, k, 1) if k else v

    flat = [e_ref[k * half : (k + 1) * half] for k in range(9)]
    terms = [flat[0:3], flat[3:6], flat[6:9]]
    both = [p + m for _, p, m in terms]
    diff = [p - m for _, p, m in terms]
    still = [s for s, _, _ in terms]
    s_ref[...] = (still[0] + both[0]) + (still[1] + both[1]) + (still[2] + both[2])
    alpha = [
        [still[0], both[0], None],
        [still[1] + still[2], both[1] + both[2], None],
        [None, None, diff[2] - diff[1]],
    ]
    beta = [
        [None, None, diff[0]],
        [None, None, diff[1] + diff[2]],
        [still[1] - still[2], both[1] - both[2], None],
    ]
    zero = jnp.zeros((half, LINE_LEN), f32)
    for b in range(3):
        for at in range(0, 2 * LINE_LEN, LINE_LEN):
            real, imag = zero, zero
            for a in range(3):
                for part in range(2):
                    k = (2 * a + part) * step - at
                    if not 0 <= k < LINE_LEN:
                        continue
                    if alpha[a][b] is not None:
                        if part == 0:
                            real = real + right(alpha[a][b], k)
                        else:
                            imag = imag + right(alpha[a][b], k)
                    elif part == 0:
                        imag = imag - right(beta[a][b], k)
                    else:
                        real = real + right(beta[a][b], k)
            m_ref[b * wide : (b + 1) * wide, at : at + LINE_LEN] = by_chunk(real, imag)


def by_chunk(real, imag):
    pieces = []
    for s in range(real.shape[0] // 2):
        pieces += [real[2 * s : 2 * s + 2], imag[2 * s : 2 * s + 2]]
    return jnp.concatenate(pieces, axis=0)


def slice_kernel(
    y_ref, m_ref, s_ref, stat_ref, other_ref, i0_ref, i1_ref, trig_ref, *send_refs
):
    n = i0_ref.shape[1]
    pixels = y_ref.shape[1]
    half = s_ref.shape[0]
    wide = 2 * half
    lane = lax.broadcasted_iota(jnp.int32, (1, LINE_LEN), 1)
    other = other_ref[...]
    other = jnp.where(lane < n, pltpu.roll(other, LINE_LEN - n, 1), pltpu.roll(other, n, 1))
    peak0, mass0 = stat_ref[0:1], stat_ref[1:2]
    peak1, mass1 = other[0:1], other[1:2]
    peak = jnp.maximum(peak0, peak1)
    grow = jnp.exp(peak0 - peak)
    scale = grow / (mass0 * grow + mass1 * jnp.exp(peak1 - peak))
    scale = jnp.where(lane < 2 * n, scale, 0.0)
    onehot = onehot_of(i0_ref, i1_ref, LINE_LEN).astype(bf16)
    share = lax.dot_general(
        (s_ref[...] * scale).astype(bf16), onehot, last_last, preferred_element_type=f32
    )
    share = by_chunk(share, jnp.zeros_like(share))
    scales = scale
    for k in range(2 * n, LINE_LEN, 2 * n):
        scales = scales + pltpu.roll(scale, k, 1)
    m = m_ref[...] * jnp.concatenate([scales, scales], axis=1)
    m = m.astype(bf16)[:, : 12 * n]
    width = 1024
    cos_row = jnp.concatenate([trig_ref[0:1]] * (width // LINE_LEN), axis=1)
    sin_row = jnp.concatenate([trig_ref[1:2]] * (width // LINE_LEN), axis=1)
    for c in range(pixels // width):
        cols = slice(c * width, (c + 1) * width)
        x = jnp.dot(m, y_ref[:, cols], preferred_element_type=f32)
        x = x[:wide] + x[wide : 2 * wide] * cos_row + x[2 * wide :] * sin_row
        for s, ref in enumerate(send_refs):
            ref[:, cols] = x[4 * s : 4 * s + 4].astype(bf16)
    for s, ref in enumerate(send_refs):
        ref[:, pixels:] = share[4 * s : 4 * s + 4].astype(bf16)


def pack_kernel(lines, cap, chunks, slot_ref, own_ref, *refs):
    recv_refs = refs[: chunks - 1]
    *send_refs, scr_ref = refs[chunks - 1 :]
    size = 2 * cap
    for l in range(lines + 1):
        cols = slice(l * LINE_LEN, (l + 1) * LINE_LEN)
        x = own_ref[:, cols].astype(f32)
        for ref in recv_refs:
            x = x + ref[:, cols].astype(f32)
        if l < lines:
            for j in range(2):
                row = j * lines + l
                scr_ref[row : row + 1, :LINE_LEN] = x[j : j + 1]
                scr_ref[row : row + 1, LINE_LEN:] = x[2 + j : 3 + j]
        else:
            tail = jnp.concatenate([x, jnp.zeros((4, LINE_LEN), f32)], axis=0)
    slots = jnp.concatenate([slot_ref[0:1], slot_ref[1:2]], axis=1)
    rows = size * len(send_refs)
    pick = slots == lax.broadcasted_iota(jnp.int32, (rows, 2 * lines), 0)
    packed = jnp.dot(
        pick.astype(f32).astype(bf16), scr_ref[...].astype(bf16), preferred_element_type=f32
    )
    for r, ref in enumerate(send_refs):
        for part in range(2):
            piece = packed[r * size : (r + 1) * size, part * LINE_LEN : (part + 1) * LINE_LEN]
            ref[part * size : (part + 1) * size] = piece.astype(ref.dtype)
        ref[2 * size :] = tail.astype(ref.dtype)


def table_kernel(lines, cap, slot_ref, table_ref, sel_ref):
    bins = table_ref.shape[0]
    sel_ref[...] = jnp.zeros(sel_ref.shape, f32)
    for l in range(lines):
        t = table_ref[:, l * LINE_LEN : (l + 1) * LINE_LEN].astype(f32)
        t = t * t
        for j in range(2):
            slot = slot_ref[j, l]

            @pl.when(slot < 2 * cap)
            def _():
                sel_ref[j, pl.ds(slot - cap * j, bins, stride=cap), :] = t


def final_kernel(cap, bins, scale, own_ref, *refs):
    *recv_refs, sel_ref, data_ref, weight_ref = refs
    x = own_ref[...].astype(f32)
    for ref in recv_refs:
        x = x + ref[...].astype(f32)
    for part in range(2):
        for j in range(2):
            row = (2 * part + j) * cap
            data_ref[0, j, part] = x[row : row + cap]
    tail = x[4 * cap :] * scale
    for j in range(2):
        total = None
        for b in range(bins):
            term = sel_ref[j, b * cap : (b + 1) * cap] * tail[j : j + 1, b : b + 1]
            total = term if b == 0 else total + term
        weight_ref[0, j] = total


def body(
    particles, defocus_bin, candidates, projections, ctf_table, inv_noise, line_slab, slab_owner
):
    n, _, pixels = particles.shape
    groups = lax.axis_size("grp")
    members = lax.axis_size("dev")
    chunks = members // 2
    lines = line_slab.shape[1]
    cap = 2 * lines // groups
    bins = ctf_table.shape[0]
    wide = 4 * chunks
    dev = lax.axis_index("dev")
    grp = lax.axis_index("grp")
    trig = jnp.asarray(trig_rows())
    noise = inv_noise[None, :]

    core = dev % 2
    chip_routes = routes(chunks, CHIP_ROUTES)
    group_routes = routes(groups, GROUP_ROUTES)

    def swap(x):
        return lax.ppermute(x, "dev", [(i, i ^ 1) for i in range(members)])

    def chip_pairs(t):
        return [(i, 2 * chip_routes[i % 2][t - 1][i // 2] + i % 2) for i in range(members)]

    def from_place(x, t):
        return lax.ppermute(x, "dev", [(j, i) for i, j in chip_pairs(t)])

    def to_place(x, t):
        return lax.ppermute(x, "dev", [(i, j ^ 1) for i, j in chip_pairs(t)])

    def to_group(x, r):
        return lax.ppermute(
            x,
            ("grp", "dev"),
            [
                (g * members + i, group_routes[i % 2][r - 1][g] * members + (i ^ 1))
                for g in range(groups)
                for i in range(members)
            ],
        )

    def at_place(t, index, table):
        return jnp.where(core == 0, lookup(index, table[0][t - 1]), lookup(index, table[1][t - 1]))

    def as_lines(x):
        count = x.shape[0]
        x = x.reshape(count, 2, lines, LINE_LEN)
        return jnp.transpose(x, (0, 2, 1, 3)).reshape(2 * count * lines, LINE_LEN)

    part0, part1 = as_lines(particles), as_lines(swap(particles))
    proj = {t: from_place(projections, t) for t in range(1, chunks)}
    proj = [as_lines(p) for p in [projections] + [proj[t] for t in range(1, chunks)]]

    vmem = pl.BlockSpec(memory_space=pltpu.VMEM)
    scratch = [pltpu.VMEM((2 * n * lines, LINE_LEN), f32), pltpu.VMEM((n, pixels), f32)]
    mark = call(
        mark_kernel, jax.ShapeDtypeStruct((8, n), jnp.int32), flops=20000000000, moved=1000
    )()
    ints0 = call(
        ints_kernel,
        jax.ShapeDtypeStruct((16, n), jnp.int32),
        in_specs=[vmem] * 3,
        moved=1000,
    )(candidates.T, defocus_bin[None, :], mark)
    ints1 = swap(ints0)
    own_rows = call(
        own_kernel,
        jax.ShapeDtypeStruct((6 * n, pixels), bf16),
        scratch_shapes=scratch,
        flops=20 * n * pixels,
        moved=32 * n * pixels,
    )(part0, ctf_table, ints0)
    y = call(
        partner_kernel,
        jax.ShapeDtypeStruct((12 * n, pixels), bf16),
        scratch_shapes=scratch,
        flops=20 * n * pixels,
        moved=32 * n * pixels,
    )(part1, ctf_table, ints1, own_rows)

    row = lax.broadcasted_iota(jnp.int32, (2 * chunks, LINE_LEN), 0)
    chip = jnp.full(row.shape, dev // 2, jnp.int32)
    for t in range(1, chunks):
        chip = jnp.where(row // 2 == t, at_place(t, dev // 2, chip_routes), chip)
    pid = 4 * chip + 2 * core + row % 2
    terms, stat = call(
        functools.partial(score_kernel, chunks),
        (
            jax.ShapeDtypeStruct((18 * chunks, LINE_LEN), f32),
            jax.ShapeDtypeStruct((8, LINE_LEN), f32),
        ),
        scratch_shapes=[
            pltpu.VMEM((4 * lines * chunks, LINE_LEN), f32),
            pltpu.VMEM((3 * wide, pixels), bf16),
            pltpu.VMEM((3 * wide, 2 * LINE_LEN), f32),
        ],
        flops=2 * 192 * 3 * wide * pixels,
        moved=30 * n * pixels,
    )(*proj, y, ctf_table, ints0, ints1, noise, trig, pid)
    line_slab, stat = lax.optimization_barrier((line_slab, stat))
    other = swap(stat)
    m, share = call(
        functools.partial(coef_kernel, n),
        (
            jax.ShapeDtypeStruct((3 * wide, 2 * LINE_LEN), f32),
            jax.ShapeDtypeStruct((2 * chunks, LINE_LEN), f32),
        ),
        flops=100000,
        moved=100000,
    )(terms)
    send = call(
        slice_kernel,
        (jax.ShapeDtypeStruct((4, pixels + LINE_LEN), bf16),) * chunks,
        flops=2 * 192 * 3 * wide * pixels,
        moved=30 * n * pixels,
    )(y, m, share, stat, other, ints0, ints1, trig)
    got = [to_place(send[t], t) for t in range(1, chunks)]
    own = swap(send[0])

    group_ids = jnp.arange(groups, dtype=jnp.int32)
    slab_hit = line_slab[:, :, None] == group_ids[None, None, :]
    owner_line = jnp.sum(jnp.where(slab_hit, slab_owner[None, None, :], 0), axis=2)
    line_ids = jnp.arange(lines, dtype=jnp.int32)
    earlier = line_ids[None, :] < line_ids[:, None]
    same_owner = owner_line[:, :, None] == owner_line[:, None, :]
    line_rank = jnp.sum(jnp.logical_and(same_owner, earlier[None]), axis=2)
    place = jnp.zeros_like(owner_line)
    for r in range(1, groups):
        place = jnp.where(owner_line == at_place(r, grp, group_routes), r, place)
    slot = (2 * cap) * place + cap * jnp.arange(2, dtype=jnp.int32)[:, None] + line_rank
    slot = slot.astype(jnp.int32)

    sel = call(
        functools.partial(table_kernel, lines, cap),
        jax.ShapeDtypeStruct((2, bins * cap, LINE_LEN), f32),
        in_specs=[pl.BlockSpec(memory_space=pltpu.SMEM), vmem],
        flops=bins * pixels,
        moved=4 * bins * pixels,
    )(slot, ctf_table)
    size = 4 * cap + 8
    send = call(
        functools.partial(pack_kernel, lines, cap, chunks),
        (jax.ShapeDtypeStruct((size, LINE_LEN), bf16),) * groups,
        scratch_shapes=[pltpu.VMEM((2 * lines, 2 * LINE_LEN), f32)],
        flops=16 * pixels,
        moved=64 * pixels,
    )(swap(slot), own, *got)
    recv = [to_group(send[r], r) for r in range(1, groups)]
    keep = swap(send[0])
    weight_scale = 2 * members / (n * groups * members)
    data, weight = (1, 2, 2, cap, LINE_LEN), (1, 2, cap, LINE_LEN)
    return call(
        functools.partial(final_kernel, cap, bins, weight_scale),
        (jax.ShapeDtypeStruct(data, f32), jax.ShapeDtypeStruct(weight, f32)),
        in_specs=[vmem] * (groups + 1),
        flops=1000,
        moved=8 * 4 * cap * LINE_LEN,
    )(keep, *recv, sel)


def solution(mesh):
    return jax.shard_map(
        body,
        mesh=mesh,
        in_specs=(
            P(("grp", "dev"), None, None),
            P(("grp", "dev")),
            P(("grp", "dev"), None),
            P("dev", None, None),
            P(),
            P(),
            P("dev", None),
            P(),
        ),
        out_specs=(P("grp", "dev", None, None, None), P("grp", "dev", None, None)),
        check_vma=False,
    )
```
